512 devices in a mesh: ch: 4 (over z_hi, core), gr: 16 (over x, y), gc: 8 (over z_lo).
Axes of the slice: x: 4, y: 4, z: 16 (z_hi: 2, z_lo: 8; z = z_hi * 8 + z_lo), core: 2. Of those that a mesh axis runs over, the one named last changes fastest.
Arguments:
- features: bfloat16 [3, 16384, 8192], P(None, ('gr', 'gc'), 'ch'), may hold values from -6 to 6
- short_taps: float32 [3, 7, 8192], P(None, None, 'ch'), may hold values from -2 to 2
- decay: float32 [16, 8192], P(None, 'ch'), may hold values from 1.5258789e-05 to 0.1, as said below
- residue: float32 [16, 8192], P(None, 'ch'), may hold values from -1 to 1
- doc_lengths: int32 [8], replicated, may hold values from 1 to 4096, 16384 in all
- gain: float32 [8192], P('ch'), may hold values from 0.5 to 1.5
Outputs:
- mixed: bfloat16 [16384, 8192], P(('gr', 'gc'), 'ch')
The draws below stay inside these ranges and needn't reach their ends.
Inputs may be any that keep to these rules, and one draw needn't show every extreme that they name: `doc_lengths`: positive lengths summing to 16384; the largest equals the stated maximum. Positive decay rates.
All inputs are finite; a program needn't handle non-finite values.
Results may differ from the reference program's by a relative error of at most 0.0077.
Values may be sent and summed in bfloat16 or wider, within the bound.
No kernel may reach another device: no remote copies, remote signals or barrier semaphores. Data moves between devices by JAX's collectives and lax.ppermute only.
A program may use at most 128 MiB of HBM per device.

```python
import math
import jax
import jax.numpy as jnp
import numpy as np
from jax import lax

D = 8192
MODES = 16
DOCS = 8
LEN = 16384


def mode_table(key):
    rate_key = jax.random.fold_in(key, 11)
    weight_key = jax.random.fold_in(key, 23)
    lowest = 1.0 / (4.0 * LEN)
    highest = 0.1
    uniform_part = jax.random.uniform(rate_key, (MODES, D), jnp.float32)
    rates = jnp.exp(jnp.log(lowest) + (jnp.log(highest) - jnp.log(lowest)) * uniform_part)
    flat_index = jnp.arange(MODES * D).reshape(MODES, D)
    rates = jnp.where(flat_index == 0, lowest, rates)
    rates = jnp.where(flat_index == 1, highest, rates)
    channel_scale = jnp.sqrt((1.0 + 2.0 * jnp.arange(D).astype(jnp.float32) / D) / 3.0)
    base = jnp.clip(0.5 * jax.random.normal(weight_key, (MODES, D), jnp.float32), -1.0, 1.0)
    weights = base * channel_scale[None, :]
    weights = jnp.where(flat_index == 2, 1.0, weights)
    weights = jnp.where(flat_index == 3, -1.0, weights)
    return (rates, weights)


def draw_decay(key, part):
    return mode_table(key)[0]


def draw_residue(key, part):
    return mode_table(key)[1]


def shard_levels(rng, dims, shards, low, high):
    loudness = 1.0
    for dim, shards_of in shards:
        steps = jax.random.uniform(jax.random.fold_in(jax.random.fold_in(rng, 6), dim), (shards_of,), jnp.float32, low / len(shards), high / len(shards))
        loudness = loudness * jnp.repeat(jnp.exp(steps), dims[dim] // shards_of).reshape((-1,) + (1,) * (len(dims) - 1 - dim))
    return loudness


def split_up(number_of, total, bound, skew):
    portions = [(1 << 20) // math.isqrt(grade ** skew) + 1 for grade in range(2, number_of + 1)]
    spare, given = total - bound - (number_of - 1), [1] * (number_of - 1)
    while spare > 0:
        free = [i for i in range(number_of - 1) if given[i] < bound]
        pool, left = sum([portions[i] for i in free]), spare
        for i in free:
            extra = min(bound - given[i], max(1, left * portions[i] // pool), spare)
            given[i] = given[i] + extra
            spare = spare - extra
    return np.array([bound] + given)


def uneven(stream_key, amount, total, bound, lean):
    if amount == 2:
        one = jax.random.randint(stream_key, (), max(1, total - bound), min(bound, total - 1) + 1)
        return jnp.stack([one, total - one])
    sizes = jnp.asarray(split_up(amount, total, bound, lean), jnp.int32)
    twos = (amount - 1) // 2
    giver, sink = sizes[1:1 + 2 * twos:2], sizes[2:2 + 2 * twos:2]
    room = jnp.minimum(giver - 1, bound - sink)
    moved = jax.random.randint(jax.random.fold_in(stream_key, 1), (twos,), 0, 1 << 20) % (room + 1)
    sizes = sizes.at[1:1 + 2 * twos:2].set(giver - moved).at[2:2 + 2 * twos:2].set(sink + moved)
    return sizes[jax.random.permutation(jax.random.fold_in(stream_key, 2), amount)]


def gaussian(key, shape, spread, limit, shards=(), held_as=jnp.bfloat16):
    result = jax.random.normal(key, shape, jnp.float32) * spread
    if len(shards) > 0:
        result = shard_levels(key, shape, shards, -0.22, 0.18) * result
    return jnp.clip(result, min=-limit, max=limit).astype(held_as)


def setup_inputs(seed: int = 0) -> dict:
    seeds = jax.random.split(jax.random.key(seed), 7)
    features = gaussian(seeds[0], (3, LEN, D), 1.0, 6.0, ((1, 128), (2, 4)))
    short_taps = gaussian(seeds[1], (3, 7, D), 7 ** -0.5, 2.0, ((2, 4),), jnp.float32)
    decay = draw_decay(jax.random.fold_in(seeds[6], 71), 0)
    residue = draw_residue(jax.random.fold_in(seeds[6], 71), 0)
    doc_lengths = uneven(seeds[4], DOCS, LEN, LEN // 4, 1).astype(jnp.int32)
    gain = jnp.clip(1.0 + 0.1 * jax.random.normal(seeds[5], (D,), jnp.float32), 0.5, 1.5)
    return dict(features=features, short_taps=short_taps, decay=decay, residue=residue, doc_lengths=doc_lengths, gain=gain)


def reference(features, short_taps, decay, residue, doc_lengths, gain):
    starts = (jnp.cumsum(doc_lengths) - doc_lengths).astype(jnp.int32)
    position = jnp.arange(LEN, dtype=jnp.int32)
    begins = lax.optimization_barrier(jnp.max(jnp.where(starts[None, :] <= position[:, None], starts[None, :], 0), axis=1)).astype(jnp.int32)
    reach = position - begins
    block_width = min(D, 512)
    block_count = D // block_width
    feat_blocks = features.reshape(3, LEN, block_count, block_width).transpose(2, 0, 1, 3)
    tap_blocks = short_taps.reshape(3, 7, block_count, block_width).transpose(2, 0, 1, 3)
    rate_blocks = decay.reshape(MODES, block_count, block_width).transpose(1, 0, 2)
    weight_blocks = residue.reshape(MODES, block_count, block_width).transpose(1, 0, 2)

    def block_pass(inputs):
        feats, taps, rates, weights = inputs
        padded = jnp.concatenate([jnp.zeros((3, 6, block_width), feats.dtype), feats], axis=1)
        summed = jnp.zeros((3, LEN, block_width), jnp.float32)
        for offset in range(7):
            window = padded[:, 6 - offset:6 - offset + LEN, :].astype(jnp.float32)
            summed = summed + jnp.where((reach >= offset)[None, :, None], taps[:, offset, None, :] * window, 0.0)
        featured = summed.astype(jnp.bfloat16)
        product = (featured[0].astype(jnp.float32) * featured[2].astype(jnp.float32)).astype(jnp.bfloat16)
        moments = jnp.arange(LEN).astype(jnp.float32)
        impulse = jnp.zeros((LEN, block_width), jnp.float32)
        for mode in range(MODES):
            impulse = impulse + weights[mode] * jnp.sqrt(2.0 * rates[mode]) * jnp.exp(-rates[mode] * moments[:, None])
        period = 2 * LEN
        spectrum = jnp.fft.rfft(product.astype(jnp.float32), n=period, axis=0) * jnp.fft.rfft(impulse, n=period, axis=0)
        conv = jnp.fft.irfft(spectrum, n=period, axis=0)[:LEN].astype(jnp.bfloat16)
        return featured[1].astype(jnp.float32) * conv.astype(jnp.float32)
    gated_blocks = lax.map(block_pass, (feat_blocks, tap_blocks, rate_blocks, weight_blocks))
    gated = gated_blocks.transpose(1, 0, 2).reshape(LEN, D)
    energy = lax.optimization_barrier(jnp.mean(gated * gated, axis=1))
    return (gated * lax.rsqrt(energy + 1e-06)[:, None] * gain[None, :]).astype(jnp.bfloat16)
```

```python
import functools

import jax
import jax.numpy as jnp
from jax import lax
from jax.experimental import pallas as pl
from jax.experimental.pallas import tpu as pltpu
from jax.sharding import PartitionSpec as P


LANES = 128
TAPS = 7
HEAD = TAPS - 1
SUB = 8
VMEM_LIMIT = 12 * 1024 * 1024


def specs(kinds):
    return [
        pl.BlockSpec(memory_space=pltpu.SMEM if k == "s" else pltpu.VMEM) for k in kinds
    ]


def doc_start(lengths, position):
    start, found = jnp.int32(0), jnp.zeros_like(position)
    for doc in range(lengths.shape[0]):
        found = jnp.where(position >= start, jnp.maximum(found, start), found)
        start = start + lengths[doc]
    return found


def short_conv(shifts, x, taps):
    tokens = x.shape[0]
    moved = jnp.dot(shifts, x, preferred_element_type=jnp.float32)
    total = x.astype(jnp.float32) * taps(0)
    for i in range(1, TAPS):
        total = total + moved[(i - 1) * tokens : i * tokens] * taps(i)
    return total.astype(jnp.bfloat16)


def rows_of(shape, dim=0):
    return lax.broadcasted_iota(jnp.int32, shape, dim)


def front_body(lengths, here, feats, taps, decay, msg, prod, shifts, stage):
    _, tokens, channels = feats.shape
    modes = decay.shape[0]
    groups = channels // LANES
    row = rows_of((tokens, tokens))
    column = rows_of((tokens, tokens), 1)
    position = row + here[0] * tokens
    reach = position - doc_start(lengths, position)
    for i in range(1, TAPS):
        hit = (column == row - i) & (reach >= i)
        shifts[(i - 1) * tokens : i * tokens, :] = jnp.where(hit, 1.0, 0.0).astype(jnp.bfloat16)
    states = groups * modes
    weights_row = rows_of((SUB, LANES)).astype(jnp.float32)
    wide = 2 * LANES
    for block in range(channels // wide):
        lanes = slice(block * wide, (block + 1) * wide)
        first, third = (
            short_conv(shifts[...], feats[b, :, lanes], lambda i, b=b: taps[b, i : i + 1, lanes])
            for b in (0, 2)
        )
        product = first.astype(jnp.float32) * third.astype(jnp.float32)
        product = jnp.where(rows_of((tokens, wide)) >= HEAD, product, 0.0).astype(jnp.bfloat16)
        prod[:, lanes] = product
        values = product.astype(jnp.float32)
        for half in range(wide // LANES):
            j = block * (wide // LANES) + half
            mine = slice(j * LANES, (j + 1) * LANES)
            v = values[:, half * LANES : (half + 1) * LANES]
            for m in range(modes):
                rate = decay[m : m + 1, mine]
                step = jnp.broadcast_to(jnp.exp(-SUB * rate), (SUB, LANES))
                state = v[0:SUB]
                for q in range(1, tokens // SUB):
                    state = state * step + v[q * SUB : (q + 1) * SUB]
                state = state * jnp.exp(-rate * (SUB - 1 - weights_row))
                end = jnp.sum(state, axis=0, keepdims=True)
                high = end.astype(jnp.bfloat16).astype(jnp.float32)
                stage[j * modes + m : j * modes + m + 1, :] = high
                stage[states + j * modes + m : states + j * modes + m + 1, :] = end - high
            at = 2 * states
            for b, low in ((0, tokens - HEAD), (2, tokens - HEAD), (1, tokens - HEAD), (0, 0), (2, 0)):
                part = feats[b, tokens - 2 * SUB : tokens, mine] if low else feats[b, 0 : 2 * SUB, mine]
                part = part.astype(jnp.float32)
                skip = 2 * SUB - HEAD if low else 0
                for r in range(HEAD):
                    stage[at + r * groups + j : at + r * groups + j + 1, :] = part[skip + r : skip + r + 1]
                at += HEAD * groups
    used = 2 * states + 5 * HEAD * groups
    if used < stage.shape[0]:
        stage[used:, :] = jnp.zeros((stage.shape[0] - used, LANES), jnp.float32)
    for c in range(stage.shape[0] // LANES):
        msg[:, c * LANES : (c + 1) * LANES] = stage[c * LANES : (c + 1) * LANES, :].T.astype(jnp.bfloat16)


def local_body(here, feats, taps, decay, residue, prod, shifts, gate, near, grow, rate_o, weight_o, taps_o, table):
    _, tokens, channels = feats.shape
    modes = decay.shape[0]
    groups = channels // LANES
    chunks = tokens // SUB
    wide = 2 * LANES
    for block in range(channels // wide):
        lanes = slice(block * wide, (block + 1) * wide)
        gate[:, lanes] = short_conv(shifts[...], feats[1, :, lanes], lambda i: taps[1, i : i + 1, lanes])
    owned = rows_of((modes, LANES), 1) == here[0]
    owned_taps = rows_of((TAPS, LANES), 1) == here[0]
    for j in range(groups):
        mine = slice(j * LANES, (j + 1) * LANES)
        at = slice(j * modes, (j + 1) * modes)
        rates, scale = decay[:, mine], residue[:, mine]
        scale = scale * jnp.sqrt(2.0 * rates)
        pick = jnp.sum(jnp.where(owned, rates, 0.0), axis=1, keepdims=True)
        rate_o[at, :] = jnp.broadcast_to(pick, (modes, LANES))
        pick = jnp.sum(jnp.where(owned, scale, 0.0), axis=1, keepdims=True)
        weight_o[at, :] = jnp.broadcast_to(pick, (modes, LANES))
        for b in range(3):
            pick = jnp.sum(jnp.where(owned_taps, taps[b, :, mine], 0.0), axis=1, keepdims=True)
            pick = jnp.broadcast_to(pick, (TAPS, LANES))
            for i in range(TAPS):
                to = (b * TAPS + i) * groups + j
                taps_o[to : to + 1, :] = pick[i : i + 1]
    inside = rows_of((SUB, LANES))
    steps = inside.astype(jnp.float32)

    def group(j, carry):
        mine = pl.ds(pl.multiple_of(j * LANES, LANES), LANES)
        sums = [jnp.zeros((SUB, LANES), jnp.float32) for _ in range(chunks)]
        for m in range(modes):
            rate = decay[m : m + 1, mine]
            weight = residue[m : m + 1, mine] * jnp.sqrt(2.0 * rate)
            step = jnp.broadcast_to(jnp.exp(-SUB * rate), (SUB, LANES))
            grow[m * SUB : (m + 1) * SUB, mine] = weight * jnp.exp(-rate * (steps + (SUB - HEAD + 1)))
            wave = weight * jnp.exp(-rate * steps)
            for q in range(chunks):
                sums[q] = sums[q] + wave
                if q + 1 < chunks:
                    wave = wave * step
        for q in range(chunks):
            table[q * SUB : (q + 1) * SUB, :] = sums[q]
        values = prod[:, mine].astype(jnp.float32)
        total = [jnp.zeros((SUB, LANES), jnp.float32) for _ in range(chunks)]
        for k in range(SUB):
            if k:
                turned = [
                    pltpu.roll(values[q * SUB : (q + 1) * SUB], k, 0) for q in range(chunks)
                ]
                low = inside < k
                moved = [
                    jnp.where(low, turned[q - 1] if q else 0.0, turned[q]) for q in range(chunks)
                ]
            else:
                moved = [values[q * SUB : (q + 1) * SUB] for q in range(chunks)]
            for d in range(chunks):
                factor = jnp.broadcast_to(table[d * SUB + k : d * SUB + k + 1, :], (SUB, LANES))
                for q in range(d, chunks):
                    total[q] = total[q] + factor * moved[q - d]
        for q in range(chunks):
            near[q * SUB : (q + 1) * SUB, mine] = total[q]
        return carry

    lax.fori_loop(0, groups, group, 0)


def owner_body(lengths, arrived, rate_o, weight_o, taps_o, back, stage, out, *, tokens):
    blocks = arrived.shape[0]
    states = rate_o.shape[0]
    groups = taps_o.shape[0] // (3 * TAPS)
    modes = states // groups
    for c in range(stage.shape[0] // LANES):
        stage[c * LANES : (c + 1) * LANES, :] = arrived[:, c * LANES : (c + 1) * LANES].astype(jnp.float32).T
    lane = rows_of((groups, blocks), 1)
    base = 2 * states

    def part(k, r):
        at = base + (k * HEAD + r) * groups
        return stage[at : at + groups, :]

    def before(k, r):
        return jnp.where(lane >= 1, pltpu.roll(part(k, r), 1, 1), 0.0)

    reach = []
    for r in range(HEAD):
        position = lane * tokens + r
        reach.append(position - doc_start(lengths, position))
    heads = []
    for last, first, b in ((0, 3, 0), (1, 4, 2)):
        ext = [before(last, r) for r in range(HEAD)] + [part(first, r) for r in range(HEAD)]
        found = []
        for r in range(HEAD):
            total = jnp.zeros((groups, blocks), jnp.float32)
            for i in range(TAPS):
                at = (b * TAPS + i) * groups
                term = taps_o[at : at + groups, :] * ext[HEAD + r - i]
                total = total + jnp.where(reach[r] >= i, term, 0.0)
            found.append(total.astype(jnp.bfloat16).astype(jnp.float32))
        heads.append(found)
    products = [(a * b).astype(jnp.bfloat16).astype(jnp.float32) for a, b in zip(*heads)]
    lane = rows_of((modes, blocks), 1)
    for j in range(groups):
        at = slice(j * modes, (j + 1) * modes)
        rate, weight = rate_o[at, :], weight_o[at, :]
        ratio = jnp.exp(-rate)
        rows = [jnp.broadcast_to(p[j : j + 1], (modes, blocks)) for p in products]
        head = rows[0]
        for r in range(1, HEAD):
            head = head * ratio + rows[r]
        total = stage[at, :] + stage[states + j * modes : states + (j + 1) * modes, :]
        total = total + jnp.exp(-rate * (tokens - HEAD)) * head
        distance = 1
        while distance < blocks:
            shifted = jnp.where(lane >= distance, pltpu.roll(total, distance, 1), 0.0)
            total = total + jnp.exp(-rate * float(tokens * distance)) * shifted
            distance *= 2
        state = jnp.where(lane >= 1, pltpu.roll(total, 1, 1), 0.0)
        for r in range(HEAD):
            state = state * ratio + rows[r]
            to = 2 * states + r * groups + j
            out[to : to + 1, :] = jnp.sum(state * weight, axis=0, keepdims=True)
        high = state.astype(jnp.bfloat16).astype(jnp.float32)
        out[at, :] = high
        out[states + j * modes : states + (j + 1) * modes, :] = state - high
    at = 2 * states + HEAD * groups
    for r in range(HEAD):
        out[at + r * groups : at + (r + 1) * groups, :] = before(2, r)
    used = 2 * states + 2 * HEAD * groups
    if used < out.shape[0]:
        out[used:, :] = jnp.zeros((out.shape[0] - used, LANES), jnp.float32)
    for c in range(out.shape[0] // LANES):
        back[:, c * LANES : (c + 1) * LANES] = out[c * LANES : (c + 1) * LANES, :].T.astype(jnp.bfloat16)


def join_body(lengths, here, back, near, gate, grow, decay, feats, taps, gated, energy, stage):
    tokens, channels = near.shape
    modes = decay.shape[0]
    groups = channels // LANES
    chunks = tokens // SUB
    states = groups * modes
    for c in range(stage.shape[0] // LANES):
        stage[c * LANES : (c + 1) * LANES, :] = back[:, c * LANES : (c + 1) * LANES].astype(jnp.float32).T
    inside = rows_of((SUB, LANES))
    position = inside + here[0] * tokens
    reach = position - doc_start(lengths, position)
    squares = [jnp.zeros((SUB, LANES), jnp.float32) for _ in range(chunks)]
    for j in range(groups):
        mine = slice(j * LANES, (j + 1) * LANES)
        total = [near[q * SUB : (q + 1) * SUB, mine] for q in range(chunks)]
        for m in range(modes):
            at = j * modes + m
            state = stage[at : at + 1, :] + stage[states + at : states + at + 1, :]
            rate = decay[m : m + 1, mine]
            step = jnp.broadcast_to(jnp.exp(-SUB * rate), (SUB, LANES))
            wave = grow[m * SUB : (m + 1) * SUB, mine] * state
            total[0] = total[0] + wave * jnp.exp(SUB * rate)
            for q in range(1, chunks):
                total[q] = total[q] + wave
                if q + 1 < chunks:
                    wave = wave * step
        at = 2 * states + j
        pieces = [stage[at + r * groups : at + r * groups + 1, :] for r in range(HEAD)]
        top = jnp.concatenate(pieces + [total[0][HEAD:SUB]], axis=0)
        total[0] = top
        at += HEAD * groups
        pieces = [stage[at + r * groups : at + r * groups + 1, :] for r in range(HEAD)]
        current = feats[1, 0 : 2 * SUB, mine].astype(jnp.float32)[0:SUB]
        ext = jnp.concatenate(pieces + [current, jnp.zeros((2, LANES), jnp.float32)], axis=0)
        front = jnp.zeros((SUB, LANES), jnp.float32)
        for i in range(TAPS):
            term = taps[1, i : i + 1, mine] * ext[HEAD - i : HEAD - i + SUB]
            front = front + jnp.where(reach >= i, term, 0.0)
        front = front.astype(jnp.bfloat16).astype(jnp.float32)
        gates = gate[:, mine].astype(jnp.float32)
        for q in range(chunks):
            g = gates[q * SUB : (q + 1) * SUB] if q else front
            value = g * total[q].astype(jnp.bfloat16).astype(jnp.float32)
            gated[q * SUB : (q + 1) * SUB, mine] = value
            squares[q] = squares[q] + value * value
    summed = jnp.sum(jnp.concatenate(squares, axis=0), axis=1, keepdims=True)
    energy[...] = jnp.broadcast_to(summed, (tokens, LANES)).T[0:1, :]


def scale_body(energy, gated, gain, mixed, *, width):
    tokens, channels = gated.shape
    scaling = lax.rsqrt(energy[...] / width + 1e-06)
    scaling = jnp.broadcast_to(scaling, (LANES, tokens)).T
    for j in range(channels // LANES):
        mine = slice(j * LANES, (j + 1) * LANES)
        mixed[:, mine] = (gated[:, mine] * scaling * gain[:, mine]).astype(jnp.bfloat16)


def exchange(block):
    blocks, width = block.shape
    moved = lax.all_to_all(
        block.reshape(blocks, 2, width // 2), ("gr", "gc"), split_axis=0, concat_axis=0, tiled=True
    )
    return moved.reshape(blocks, width)


def padded(rows):
    return -(-rows // (2 * LANES)) * 2 * LANES


def per_device(features, short_taps, decay, residue, doc_lengths, gain):
    _, tokens, channels = features.shape
    modes = decay.shape[0]
    blocks = lax.axis_size(("gr", "gc"))
    groups = channels // LANES
    states = groups * modes
    here = lax.axis_index(("gr", "gc")).astype(jnp.int32).reshape(1)
    f32, bf16 = jnp.float32, jnp.bfloat16
    sds = jax.ShapeDtypeStruct
    out_rows = padded(2 * states + 5 * HEAD * groups)
    msg, prod, shifts = pl.pallas_call(
        front_body,
        out_shape=(
            sds((blocks, out_rows), bf16),
            sds((tokens, channels), bf16),
            sds((HEAD * tokens, tokens), bf16),
        ),
        in_specs=specs("ssvvv"),
        out_specs=specs("vvv"),
        scratch_shapes=[pltpu.VMEM((out_rows, LANES), f32)],
        compiler_params=pltpu.CompilerParams(vmem_limit_bytes=VMEM_LIMIT),
        cost_estimate=pl.CostEstimate(flops=10**7, bytes_accessed=4 * 10**6, transcendentals=0),
        name="front",
    )(doc_lengths, here, features, short_taps, decay)
    arrived = exchange(msg)
    gate, near, grow, rate_o, weight_o, taps_o = pl.pallas_call(
        local_body,
        out_shape=(
            sds((tokens, channels), bf16),
            sds((tokens, channels), f32),
            sds((modes * SUB, channels), f32),
            sds((states, LANES), f32),
            sds((states, LANES), f32),
            sds((3 * TAPS * groups, LANES), f32),
        ),
        in_specs=specs("svvvvvv"),
        out_specs=specs("vvvvvv"),
        scratch_shapes=[pltpu.VMEM((tokens, LANES), f32)],
        compiler_params=pltpu.CompilerParams(vmem_limit_bytes=VMEM_LIMIT),
        cost_estimate=pl.CostEstimate(flops=10**8, bytes_accessed=8 * 10**6, transcendentals=0),
        name="local",
    )(here, features, short_taps, decay, residue, prod, shifts)
    back_rows = padded(2 * states + 2 * HEAD * groups)
    back = pl.pallas_call(
        functools.partial(owner_body, tokens=tokens),
        out_shape=sds((blocks, back_rows), bf16),
        in_specs=specs("svvvv"),
        out_specs=specs("v")[0],
        scratch_shapes=[pltpu.VMEM((out_rows, LANES), f32), pltpu.VMEM((back_rows, LANES), f32)],
        compiler_params=pltpu.CompilerParams(vmem_limit_bytes=VMEM_LIMIT),
        cost_estimate=pl.CostEstimate(flops=10**6, bytes_accessed=10**6, transcendentals=0),
        name="owner",
    )(doc_lengths, arrived, rate_o, weight_o, taps_o)
    given = exchange(back)
    gated, energy = pl.pallas_call(
        join_body,
        out_shape=(sds((tokens, channels), f32), sds((1, tokens), f32)),
        in_specs=specs("ssvvvvvvv"),
        out_specs=specs("vv"),
        scratch_shapes=[pltpu.VMEM((back_rows, LANES), f32)],
        compiler_params=pltpu.CompilerParams(vmem_limit_bytes=VMEM_LIMIT),
        cost_estimate=pl.CostEstimate(flops=10**7, bytes_accessed=5 * 10**6, transcendentals=0),
        name="join",
    )(doc_lengths, here, given, near, gate, grow, decay, features, short_taps)
    energy = lax.psum(energy, "ch")
    width = float(channels * lax.axis_size("ch"))
    return pl.pallas_call(
        functools.partial(scale_body, width=width),
        out_shape=sds((tokens, channels), bf16),
        in_specs=specs("vvv"),
        out_specs=specs("v")[0],
        compiler_params=pltpu.CompilerParams(vmem_limit_bytes=VMEM_LIMIT),
        cost_estimate=pl.CostEstimate(flops=10**6, bytes_accessed=2 * 10**6, transcendentals=0),
        name="scale",
    )(energy, gated, gain.reshape(1, channels))


def solution(mesh):
    placed = (
        P(None, ("gr", "gc"), "ch"),
        P(None, None, "ch"),
        P(None, "ch"),
        P(None, "ch"),
        P(),
        P("ch"),
    )
    return jax.shard_map(
        per_device, mesh=mesh, in_specs=placed, out_specs=P(("gr", "gc"), "ch"), check_vma=False
    )
```

```python
import functools

import jax
import jax.numpy as jnp
from jax import lax
from jax.experimental import pallas as pl
from jax.experimental.pallas import tpu as pltpu
from jax.sharding import PartitionSpec as P


LANES = 128
TAPS = 7
HEAD = TAPS - 1
SUB = 8
VMEM_LIMIT = 12 * 1024 * 1024


def doc_start(lengths, position):
    start, found = jnp.int32(0), jnp.zeros_like(position)
    for doc in range(lengths.shape[0]):
        found = jnp.where(position >= start, jnp.maximum(found, start), found)
        start = start + lengths[doc]
    return found


def short_conv(shifts, x, taps):
    tokens = x.shape[0]
    moved = jnp.dot(shifts, x, preferred_element_type=jnp.float32)
    total = x.astype(jnp.float32) * taps(0)
    for i in range(1, TAPS):
        total = total + moved[(i - 1) * tokens : i * tokens] * taps(i)
    return total.astype(jnp.bfloat16)


def rows_of(shape, dim=0):
    return lax.broadcasted_iota(jnp.int32, shape, dim)


def powers(ratio):
    square = ratio * ratio
    fourth = square * square
    return ratio, square, fourth, fourth * fourth


def spread(row, rows=SUB):
    return jnp.broadcast_to(row, (rows, row.shape[1]))


def fill_shifts(shifts, lengths, first_token):
    tokens = shifts.shape[1]
    row = rows_of((tokens, tokens))
    column = rows_of((tokens, tokens), 1)
    position = row + first_token
    reach = position - doc_start(lengths, position)
    for i in range(1, TAPS):
        hit = (column == row - i) & (reach >= i)
        shifts[(i - 1) * tokens : i * tokens, :] = jnp.where(hit, 1.0, 0.0).astype(jnp.bfloat16)


def front_body(
    lengths_hbm, here, feats_hbm, taps_hbm, decay_hbm, msg, prod_hbm, stage, feats, taps, decay, prod, shifts, lengths, sems
):
    _, tokens, channels = feats.shape
    modes = decay.shape[0]
    groups = channels // LANES
    wide = 2 * LANES
    count = channels // wide

    def fetched(block):
        lanes = slice(block * wide, (block + 1) * wide)
        return pltpu.make_async_copy(feats_hbm.at[:, :, lanes], feats.at[:, :, lanes], sems.at[3 + block])

    def stored(block):
        lanes = slice(block * wide, (block + 1) * wide)
        return pltpu.make_async_copy(prod.at[:, lanes], prod_hbm.at[:, lanes], sems.at[3 + count + block])

    counted = pltpu.make_async_copy(lengths_hbm, lengths, sems.at[0])
    others = (
        pltpu.make_async_copy(taps_hbm, taps, sems.at[1]),
        pltpu.make_async_copy(decay_hbm, decay, sems.at[2]),
    )
    counted.start()
    fetched(0).start()
    for copy in others:
        copy.start()
    for block in range(1, count):
        fetched(block).start()
    states = groups * modes
    used = states + 5 * HEAD * groups
    if used < stage.shape[0]:
        stage[used:, :] = jnp.zeros((stage.shape[0] - used, LANES), jnp.float32)
    counted.wait()
    fill_shifts(shifts, lengths, here[0] * tokens)
    for copy in others:
        copy.wait()
    for block in range(count):
        lanes = slice(block * wide, (block + 1) * wide)
        fetched(block).wait()
        first, third = (
            short_conv(shifts[...], feats[b, :, lanes], lambda i, b=b: taps[b, i : i + 1, lanes])
            for b in (0, 2)
        )
        product = first.astype(jnp.float32) * third.astype(jnp.float32)
        product = jnp.where(rows_of((tokens, wide)) >= HEAD, product, 0.0).astype(jnp.bfloat16)
        prod[:, lanes] = product
        stored(block).start()
        values = product.astype(jnp.float32)
        for half in range(wide // LANES):
            j = block * (wide // LANES) + half
            mine = slice(j * LANES, (j + 1) * LANES)
            v = values[:, half * LANES : (half + 1) * LANES]
            tables = powers(jnp.exp(-decay[:, mine]))
            for m in range(modes):
                one, two, four, eight = (spread(t[m : m + 1]) for t in tables)
                state = v[0:SUB]
                for q in range(1, tokens // SUB):
                    state = state * eight + v[q * SUB : (q + 1) * SUB]
                state = state * four + pltpu.roll(state, SUB - 4, 0)
                state = state * two + pltpu.roll(state, SUB - 2, 0)
                state = state * one + pltpu.roll(state, SUB - 1, 0)
                stage[j * modes + m : j * modes + m + 1, :] = state[0:1]
            at = states
            for b, low in ((0, True), (2, True), (1, True), (0, False), (2, False)):
                part = feats[b, tokens - 2 * SUB : tokens, mine] if low else feats[b, 0 : 2 * SUB, mine]
                part = part.astype(jnp.float32)
                skip = 2 * SUB - HEAD if low else 0
                for r in range(HEAD):
                    stage[at + r * groups + j : at + r * groups + j + 1, :] = part[skip + r : skip + r + 1]
                at += HEAD * groups
    for c in range(stage.shape[0] // LANES):
        msg[:, c * LANES : (c + 1) * LANES] = stage[c * LANES : (c + 1) * LANES, :].T.astype(jnp.bfloat16)
    for block in range(count):
        stored(block).wait()


def local_body(
    lengths, here, feats_hbm, prod_hbm, taps, decay, residue, gate, near, edge, owned, table, feats, prod, shifts, sems
):
    tokens, channels = feats.shape
    modes = decay.shape[0]
    copies = (
        pltpu.make_async_copy(feats_hbm.at[1], feats, sems.at[0]),
        pltpu.make_async_copy(prod_hbm, prod, sems.at[1]),
    )
    for copy in copies:
        copy.start()
    fill_shifts(shifts, lengths, here[0] * tokens)
    for copy in copies:
        copy.wait()
    groups = channels // LANES
    chunks = tokens // SUB
    wide = 2 * LANES
    for block in range(channels // wide):
        lanes = slice(block * wide, (block + 1) * wide)
        gate[:, lanes] = short_conv(shifts[...], feats[:, lanes], lambda i: taps[1, i : i + 1, lanes])
    states = groups * modes
    edge[...] = feats[0 : 2 * SUB, :].astype(jnp.float32)[0:SUB]
    chosen = rows_of((modes, LANES), 1) == here[0]
    chosen_taps = rows_of((TAPS, LANES), 1) == here[0]
    for j in range(groups):
        mine = slice(j * LANES, (j + 1) * LANES)
        at = slice(j * modes, (j + 1) * modes)
        rates, scale = decay[:, mine], residue[:, mine]
        scale = scale * jnp.sqrt(2.0 * rates)
        pick = jnp.sum(jnp.where(chosen, rates, 0.0), axis=1, keepdims=True)
        owned[at, :] = jnp.broadcast_to(pick, (modes, LANES))
        pick = jnp.sum(jnp.where(chosen, scale, 0.0), axis=1, keepdims=True)
        owned[states + j * modes : states + (j + 1) * modes, :] = jnp.broadcast_to(pick, (modes, LANES))
        for b in range(3):
            pick = jnp.sum(jnp.where(chosen_taps, taps[b, :, mine], 0.0), axis=1, keepdims=True)
            pick = jnp.broadcast_to(pick, (TAPS, LANES))
            for i in range(TAPS):
                to = 2 * states + (b * TAPS + i) * groups + j
                owned[to : to + 1, :] = pick[i : i + 1]
    inside = rows_of((SUB, LANES))
    steps = inside.astype(jnp.float32)

    def group(j, carry):
        mine = pl.ds(pl.multiple_of(j * LANES, LANES), LANES)
        sums = [jnp.zeros((SUB, LANES), jnp.float32) for _ in range(chunks)]
        for m in range(modes):
            rate = decay[m : m + 1, mine]
            weight = residue[m : m + 1, mine] * jnp.sqrt(2.0 * rate)
            step = jnp.broadcast_to(jnp.exp(-SUB * rate), (SUB, LANES))
            wave = weight * jnp.exp(-rate * steps)
            for q in range(chunks):
                sums[q] = sums[q] + wave
                if q + 1 < chunks:
                    wave = wave * step
        for q in range(chunks):
            table[q * SUB : (q + 1) * SUB, :] = sums[q]
        values = prod[:, mine].astype(jnp.float32)
        total = [jnp.zeros((SUB, LANES), jnp.float32) for _ in range(chunks)]
        for k in range(SUB):
            if k:
                turned = [
                    pltpu.roll(values[q * SUB : (q + 1) * SUB], k, 0) for q in range(chunks)
                ]
                low = inside < k
                moved = [
                    jnp.where(low, turned[q - 1] if q else 0.0, turned[q]) for q in range(chunks)
                ]
            else:
                moved = [values[q * SUB : (q + 1) * SUB] for q in range(chunks)]
            for d in range(chunks):
                factor = jnp.broadcast_to(table[d * SUB + k : d * SUB + k + 1, :], (SUB, LANES))
                for q in range(d, chunks):
                    total[q] = total[q] + factor * moved[q - d]
        for q in range(chunks):
            near[q * SUB : (q + 1) * SUB, mine] = total[q]
        return carry

    lax.fori_loop(0, groups, group, 0)


def owner_body(lengths, arrived, owned, back, stage, out, *, tokens, modes):
    blocks = arrived.shape[0]
    groups = owned.shape[0] // (2 * modes + 3 * TAPS)
    states = modes * groups
    for c in range(stage.shape[0] // LANES):
        stage[c * LANES : (c + 1) * LANES, :] = arrived[:, c * LANES : (c + 1) * LANES].astype(jnp.float32).T
    lane = rows_of((groups, blocks), 1)

    def part(k, r):
        at = states + (k * HEAD + r) * groups
        return stage[at : at + groups, :]

    def before(k, r):
        return jnp.where(lane >= 1, pltpu.roll(part(k, r), 1, 1), 0.0)

    reach = []
    for r in range(HEAD):
        position = lane * tokens + r
        reach.append(position - doc_start(lengths, position))
    heads = []
    for last, first, b in ((0, 3, 0), (1, 4, 2)):
        ext = [before(last, r) for r in range(HEAD)] + [part(first, r) for r in range(HEAD)]
        found = []
        for r in range(HEAD):
            total = jnp.zeros((groups, blocks), jnp.float32)
            for i in range(TAPS):
                at = 2 * states + (b * TAPS + i) * groups
                term = owned[at : at + groups, :] * ext[HEAD + r - i]
                total = total + jnp.where(reach[r] >= i, term, 0.0)
            found.append(total.astype(jnp.bfloat16).astype(jnp.float32))
        heads.append(found)
    products = [(a * b).astype(jnp.bfloat16).astype(jnp.float32) for a, b in zip(*heads)]
    lane = rows_of((modes, blocks), 1)
    for j in range(groups):
        at = slice(j * modes, (j + 1) * modes)
        rate, weight = owned[at, :], owned[states + j * modes : states + (j + 1) * modes, :]
        ratio = jnp.exp(-rate)
        rows = [spread(p[j : j + 1], modes) for p in products]
        head = rows[0]
        for r in range(1, HEAD):
            head = head * ratio + rows[r]
        total = stage[at, :] + jnp.exp(-rate * (tokens - HEAD)) * head
        decline = jnp.exp(-rate * tokens)
        distance = 1
        while distance < blocks:
            shifted = jnp.where(lane >= distance, pltpu.roll(total, distance, 1), 0.0)
            total = total + decline * shifted
            decline = decline * decline
            distance *= 2
        state = jnp.where(lane >= 1, pltpu.roll(total, 1, 1), 0.0)
        for r in range(HEAD):
            state = state * ratio + rows[r]
            to = states + r * groups + j
            out[to : to + 1, :] = jnp.sum(state * weight, axis=0, keepdims=True)
        out[at, :] = state
    at = states + HEAD * groups
    for r in range(HEAD):
        out[at + r * groups : at + (r + 1) * groups, :] = before(2, r)
    used = states + 2 * HEAD * groups
    if used < out.shape[0]:
        out[used:, :] = jnp.zeros((out.shape[0] - used, LANES), jnp.float32)
    for c in range(out.shape[0] // LANES):
        back[:, c * LANES : (c + 1) * LANES] = out[c * LANES : (c + 1) * LANES, :].T.astype(jnp.bfloat16)


def join_body(lengths, here, back, near, gate, edge, decay, residue, taps, gated, energy, stage):
    tokens, channels = near.shape
    modes = decay.shape[0]
    groups = channels // LANES
    chunks = tokens // SUB
    states = groups * modes
    for c in range(stage.shape[0] // LANES):
        stage[c * LANES : (c + 1) * LANES, :] = back[:, c * LANES : (c + 1) * LANES].astype(jnp.float32).T
    inside = rows_of((SUB, LANES))
    position = inside + here[0] * tokens
    reach = position - doc_start(lengths, position)
    odd, pair, quad = ((inside & bit) != 0 for bit in (1, 2, 4))
    squares = [jnp.zeros((SUB, LANES), jnp.float32) for _ in range(chunks)]
    for j in range(groups):
        mine = slice(j * LANES, (j + 1) * LANES)
        total = [near[q * SUB : (q + 1) * SUB, mine] for q in range(chunks)]
        rates = decay[:, mine]
        tables = powers(jnp.exp(-rates))
        start = stage[j * modes : (j + 1) * modes, :] * residue[:, mine] * jnp.sqrt(2.0 * rates)
        start = start * tables[0] * tables[1]
        grown = jnp.exp(SUB * rates)
        for m in range(modes):
            one, two, four, eight = (spread(t[m : m + 1]) for t in tables)
            wave = spread(start[m : m + 1])
            wave = jnp.where(odd, wave * one, wave)
            wave = jnp.where(pair, wave * two, wave)
            wave = jnp.where(quad, wave * four, wave)
            total[0] = total[0] + wave * spread(grown[m : m + 1])
            for q in range(1, chunks):
                total[q] = total[q] + wave
                if q + 1 < chunks:
                    wave = wave * eight
        at = states + j
        pieces = [stage[at + r * groups : at + r * groups + 1, :] for r in range(HEAD)]
        total[0] = jnp.concatenate(pieces + [total[0][HEAD:SUB]], axis=0)
        at += HEAD * groups
        pieces = [stage[at + r * groups : at + r * groups + 1, :] for r in range(HEAD)]
        ext = jnp.concatenate(pieces + [edge[:, mine], jnp.zeros((2, LANES), jnp.float32)], axis=0)
        front = jnp.zeros((SUB, LANES), jnp.float32)
        for i in range(TAPS):
            term = taps[1, i : i + 1, mine] * ext[HEAD - i : HEAD - i + SUB]
            front = front + jnp.where(reach >= i, term, 0.0)
        front = front.astype(jnp.bfloat16).astype(jnp.float32)
        gates = gate[:, mine].astype(jnp.float32)
        for q in range(chunks):
            g = gates[q * SUB : (q + 1) * SUB] if q else front
            value = g * total[q].astype(jnp.bfloat16).astype(jnp.float32)
            gated[q * SUB : (q + 1) * SUB, mine] = value
            squares[q] = squares[q] + value * value
    summed = jnp.sum(jnp.concatenate(squares, axis=0), axis=1, keepdims=True)
    row = jnp.broadcast_to(summed, (tokens, LANES)).T[0:1, :]
    for k in range(energy.shape[0]):
        energy[k : k + 1, :] = row


def scale_body(energy, gated, gain, mixed, *, width):
    tokens, channels = gated.shape
    scaling = lax.rsqrt(jnp.sum(energy[...], axis=0, keepdims=True) / width + 1e-06)
    scaling = jnp.broadcast_to(scaling, (LANES, tokens)).T
    for j in range(channels // LANES):
        mine = slice(j * LANES, (j + 1) * LANES)
        mixed[:, mine] = (gated[:, mine] * scaling * gain[:, mine]).astype(jnp.bfloat16)


def exchange(block):
    blocks, width = block.shape
    moved = lax.all_to_all(
        block.reshape(blocks, 2, width // 2), ("gr", "gc"), split_axis=0, concat_axis=0, tiled=True
    )
    return moved.reshape(blocks, width)


def padded(rows):
    return -(-rows // (2 * LANES)) * 2 * LANES


def kernel(body, name, kinds, outs, scratch, flops, moved, given="vvvv"):
    spaces = {"s": pltpu.SMEM, "v": pltpu.VMEM, "h": pltpu.HBM}
    return pl.pallas_call(
        body,
        out_shape=outs,
        in_specs=[pl.BlockSpec(memory_space=spaces[k]) for k in kinds],
        out_specs=tuple(pl.BlockSpec(memory_space=spaces[k]) for k, _ in zip(given, outs)),
        scratch_shapes=scratch,
        compiler_params=pltpu.CompilerParams(vmem_limit_bytes=VMEM_LIMIT),
        cost_estimate=pl.CostEstimate(flops=flops, bytes_accessed=moved, transcendentals=0),
        name=name,
    )


def per_device(features, short_taps, decay, residue, doc_lengths, gain):
    _, tokens, channels = features.shape
    modes = decay.shape[0]
    blocks = lax.axis_size(("gr", "gc"))
    groups = channels // LANES
    states = groups * modes
    here = lax.axis_index(("gr", "gc")).astype(jnp.int32).reshape(1)
    f32, bf16 = jnp.float32, jnp.bfloat16
    sds = jax.ShapeDtypeStruct
    vmem = pltpu.VMEM
    out_rows = padded(states + 5 * HEAD * groups)
    back_rows = padded(states + 2 * HEAD * groups)
    front = kernel(
        front_body,
        "front",
        "hshhh",
        (sds((blocks, out_rows), bf16), sds((tokens, channels), bf16)),
        [
            vmem((out_rows, LANES), f32),
            vmem(features.shape, bf16),
            vmem(short_taps.shape, f32),
            vmem(decay.shape, f32),
            vmem((tokens, channels), bf16),
            vmem((HEAD * tokens, tokens), bf16),
            pltpu.SMEM(doc_lengths.shape, jnp.int32),
            pltpu.SemaphoreType.DMA((3 + 2 * (channels // (2 * LANES)),)),
        ],
        10**7,
        4 * 10**6,
        "vh",
    )
    far = functools.partial(pltpu.with_memory_space_constraint, memory_space=pltpu.HBM)
    msg, prod = front(far(doc_lengths), here, far(features), far(short_taps), far(decay))
    arrived = exchange(msg)
    local = kernel(
        local_body,
        "local",
        "sshhvvv",
        (
            sds((tokens, channels), bf16),
            sds((tokens, channels), f32),
            sds((SUB, channels), f32),
            sds((2 * states + 3 * TAPS * groups, LANES), f32),
        ),
        [
            vmem((tokens, LANES), f32),
            vmem((tokens, channels), bf16),
            vmem((tokens, channels), bf16),
            vmem((HEAD * tokens, tokens), bf16),
            pltpu.SemaphoreType.DMA((2,)),
        ],
        10**8,
        8 * 10**6,
    )
    gate, near, edge, owned = local(doc_lengths, here, far(features), far(prod), short_taps, decay, residue)
    owner = kernel(
        functools.partial(owner_body, tokens=tokens, modes=modes),
        "owner",
        "svv",
        (sds((blocks, back_rows), bf16),),
        [vmem((out_rows, LANES), f32), vmem((back_rows, LANES), f32)],
        10**6,
        10**6,
    )
    given = exchange(owner(doc_lengths, arrived, owned)[0])
    parts = lax.axis_size("ch")
    join = kernel(
        join_body,
        "join",
        "ssvvvvvvv",
        (sds((tokens, channels), f32), sds((parts, tokens), f32)),
        [vmem((back_rows, LANES), f32)],
        10**7,
        5 * 10**6,
    )
    gated, energy = join(doc_lengths, here, given, near, gate, edge, decay, residue, short_taps)
    energy = lax.all_to_all(energy.reshape(parts, 1, tokens), "ch", split_axis=0, concat_axis=0, tiled=True)
    scale = kernel(
        functools.partial(scale_body, width=float(channels * parts)),
        "scale",
        "vvv",
        (sds((tokens, channels), bf16),),
        [],
        10**6,
        2 * 10**6,
    )
    return scale(energy.reshape(parts, tokens), gated, gain.reshape(1, channels))[0]


def solution(mesh):
    placed = (
        P(None, ("gr", "gc"), "ch"),
        P(None, None, "ch"),
        P(None, "ch"),
        P(None, "ch"),
        P(),
        P("ch"),
    )
    return jax.shard_map(
        per_device, mesh=mesh, in_specs=placed, out_specs=P(("gr", "gc"), "ch"), check_vma=False
    )
```

```python
import functools

import jax
import jax.numpy as jnp
from jax import lax
from jax.experimental import pallas as pl
from jax.experimental.pallas import tpu as pltpu
from jax.sharding import PartitionSpec as P


LANES = 128
TAPS = 7
HEAD = TAPS - 1
SUB = 8
VMEM_LIMIT = 12 * 1024 * 1024


def doc_start(lengths, position):
    start, found = jnp.int32(0), jnp.zeros_like(position)
    for doc in range(lengths.shape[0]):
        found = jnp.where(position >= start, jnp.maximum(found, start), found)
        start = start + lengths[doc]
    return found


def short_conv(shifts, x, taps):
    tokens = x.shape[0]
    moved = jnp.dot(shifts, x, preferred_element_type=jnp.float32)
    total = x.astype(jnp.float32) * taps(0)
    for i in range(1, TAPS):
        total = total + moved[(i - 1) * tokens : i * tokens] * taps(i)
    return total.astype(jnp.bfloat16)


def rows_of(shape, dim=0):
    return lax.broadcasted_iota(jnp.int32, shape, dim)


def powers(ratio):
    square = ratio * ratio
    fourth = square * square
    return ratio, square, fourth, fourth * fourth


def spread(row, rows=SUB):
    return jnp.broadcast_to(row, (rows, row.shape[1]))


def fill_shifts(shifts, lengths, first_token):
    tokens = shifts.shape[1]
    row = rows_of((tokens, tokens))
    column = rows_of((tokens, tokens), 1)
    position = row + first_token
    reach = position - doc_start(lengths, position)
    for i in range(1, TAPS):
        hit = (column == row - i) & (reach >= i)
        shifts[(i - 1) * tokens : i * tokens, :] = jnp.where(hit, 1.0, 0.0).astype(jnp.bfloat16)


def front_body(
    lengths_hbm, here, feats_hbm, taps_hbm, decay_hbm, msg, prod_hbm, stage, feats, taps, decay, prod, shifts, lengths, sems
):
    pair, tokens, channels = feats.shape
    modes = decay.shape[0]
    groups = channels // LANES
    wide = 2 * LANES
    count = channels // wide

    def fetched(block, k):
        lanes = slice(block * wide, (block + 1) * wide)
        at = 3 + count + block * pair + k
        return pltpu.make_async_copy(feats_hbm.at[2 * k, :, lanes], feats.at[k, :, lanes], sems.at[at])

    def stored(block):
        lanes = slice(block * wide, (block + 1) * wide)
        return pltpu.make_async_copy(prod.at[:, lanes], prod_hbm.at[:, lanes], sems.at[3 + block])

    counted = pltpu.make_async_copy(lengths_hbm, lengths, sems.at[0])
    others = (
        pltpu.make_async_copy(taps_hbm, taps, sems.at[1]),
        pltpu.make_async_copy(decay_hbm, decay, sems.at[2]),
    )
    counted.start()
    for k in range(pair):
        fetched(0, k).start()
    for copy in others:
        copy.start()
    for block in range(1, count):
        for k in range(pair):
            fetched(block, k).start()
    states = groups * modes
    used = states + 2 * pair * HEAD * groups
    if used < stage.shape[0]:
        stage[used:, :] = jnp.zeros((stage.shape[0] - used, LANES), jnp.float32)
    counted.wait()
    fill_shifts(shifts, lengths, here[0] * tokens)
    for copy in others:
        copy.wait()
    for block in range(count):
        lanes = slice(block * wide, (block + 1) * wide)
        for k in range(pair):
            fetched(block, k).wait()
        first, third = (
            short_conv(shifts[...], feats[k, :, lanes], lambda i, k=k: taps[2 * k, i : i + 1, lanes])
            for k in range(pair)
        )
        product = first.astype(jnp.float32) * third.astype(jnp.float32)
        product = jnp.where(rows_of((tokens, wide)) >= HEAD, product, 0.0).astype(jnp.bfloat16)
        prod[:, lanes] = product
        stored(block).start()
        values = product.astype(jnp.float32)
        for half in range(wide // LANES):
            j = block * (wide // LANES) + half
            mine = slice(j * LANES, (j + 1) * LANES)
            v = values[:, half * LANES : (half + 1) * LANES]
            tables = powers(jnp.exp(-decay[:, mine]))
            for m in range(modes):
                one, two, four, eight = (spread(t[m : m + 1]) for t in tables)
                state = v[0:SUB]
                for q in range(1, tokens // SUB):
                    state = state * eight + v[q * SUB : (q + 1) * SUB]
                state = state * four + pltpu.roll(state, SUB - 4, 0)
                state = state * two + pltpu.roll(state, SUB - 2, 0)
                state = state * one + pltpu.roll(state, SUB - 1, 0)
                stage[j * modes + m : j * modes + m + 1, :] = state[0:1]
            at = states
            for k, low in ((0, True), (1, True), (0, False), (1, False)):
                part = feats[k, tokens - 2 * SUB : tokens, mine] if low else feats[k, 0 : 2 * SUB, mine]
                part = part.astype(jnp.float32)
                skip = 2 * SUB - HEAD if low else 0
                for r in range(HEAD):
                    stage[at + r * groups + j : at + r * groups + j + 1, :] = part[skip + r : skip + r + 1]
                at += HEAD * groups
    for c in range(stage.shape[0] // LANES):
        msg[:, c * LANES : (c + 1) * LANES] = stage[c * LANES : (c + 1) * LANES, :].T.astype(jnp.bfloat16)
    for block in range(count):
        stored(block).wait()


def gate_body(lengths, here, feats_hbm, taps, decay, residue, gate, ends, owned, feats, shifts, sems):
    _, tokens, channels = feats.shape
    modes = decay.shape[0]
    groups = channels // LANES
    wide = 2 * LANES
    copies = [
        pltpu.make_async_copy(feats_hbm.at[b], feats.at[b], sems.at[b]) for b in (1, 0, 2)
    ]
    for copy in copies:
        copy.start()
    fill_shifts(shifts, lengths, here[0] * tokens)
    states = groups * modes
    chosen = rows_of((modes, LANES), 1) == here[0]
    chosen_taps = rows_of((TAPS, LANES), 1) == here[0]
    for j in range(groups):
        mine = slice(j * LANES, (j + 1) * LANES)
        at = slice(j * modes, (j + 1) * modes)
        pick = jnp.sum(jnp.where(chosen, decay[:, mine], 0.0), axis=1, keepdims=True)
        owned[at, :] = jnp.broadcast_to(pick, (modes, LANES))
        for b in (0, 2):
            pick = jnp.sum(jnp.where(chosen_taps, taps[b, :, mine], 0.0), axis=1, keepdims=True)
            pick = jnp.broadcast_to(pick, (TAPS, LANES))
            for i in range(TAPS):
                to = states + (b // 2 * TAPS + i) * groups + j
                owned[to : to + 1, :] = pick[i : i + 1]
    for copy in copies:
        copy.wait()
    for b in range(3):
        ends[b] = feats[b, tokens - 2 * SUB : tokens, :].astype(jnp.float32)[SUB:].astype(jnp.bfloat16)
    for block in range(channels // wide):
        lanes = slice(block * wide, (block + 1) * wide)
        gate[:, lanes] = short_conv(shifts[...], feats[1, :, lanes], lambda i: taps[1, i : i + 1, lanes])


def near_body(
    lengths, here, turn, halo, feats_hbm, prod_hbm, taps, decay, residue, near, top, table, prod, front, last, sems
):
    tokens, channels = near.shape
    modes = decay.shape[0]
    groups = channels // LANES
    chunks = tokens // SUB
    copies = [
        pltpu.make_async_copy(feats_hbm.at[b, 0 : 2 * SUB, :], front.at[b], sems.at[b]) for b in range(3)
    ]
    copies.append(pltpu.make_async_copy(prod_hbm, prod, sems.at[3]))
    for copy in copies:
        copy.start()
    last[...] = halo[...].astype(jnp.float32)
    inside = rows_of((SUB, LANES))
    steps = inside.astype(jnp.float32)
    position = inside + here[0] * tokens
    reach = position - doc_start(lengths, position)
    for copy in copies:
        copy.wait()

    def head(b, mine):
        now = front[b, :, mine].astype(jnp.float32)[0:SUB]
        before = last[b, :, mine]
        total = now * taps[b, 0:1, mine]
        for i in range(1, TAPS):
            moved = jnp.where(inside < i, pltpu.roll(before, i, 0), pltpu.roll(now, i, 0))
            total = total + jnp.where(reach >= i, moved * taps[b, i : i + 1, mine], 0.0)
        return total.astype(jnp.bfloat16).astype(jnp.float32)

    def group(j, carry):
        mine = pl.ds(pl.multiple_of(j * LANES, LANES), LANES)
        top[:, mine] = head(1, mine)
        first = (head(0, mine) * head(2, mine)).astype(jnp.bfloat16).astype(jnp.float32)
        sums = [jnp.zeros((SUB, LANES), jnp.float32) for _ in range(chunks)]
        rates = decay[:, mine]
        weights = residue[:, mine] * jnp.sqrt(2.0 * rates)
        eights = jnp.exp(-SUB * rates)
        for m in range(modes):
            step = spread(eights[m : m + 1])
            wave = weights[m : m + 1] * jnp.exp(-rates[m : m + 1] * steps)
            for q in range(chunks):
                sums[q] = sums[q] + wave
                if q + 1 < chunks:
                    wave = wave * step
        for q in range(chunks):
            table[q * SUB : (q + 1) * SUB, :] = sums[q]
        values = prod[:, mine].astype(jnp.float32)
        values = [values[q * SUB : (q + 1) * SUB] for q in range(chunks)]
        values[0] = jnp.where(inside < HEAD, first, values[0])
        total = [jnp.zeros((SUB, LANES), jnp.float32) for _ in range(chunks)]
        for k in range(SUB):
            moved = values
            if k:
                turned = [pltpu.roll(v, k, 0) for v in values]
                low = inside < k
                moved = [jnp.where(low, turned[q - 1] if q else 0.0, turned[q]) for q in range(chunks)]
            for d in range(chunks):
                factor = spread(table[d * SUB + k : d * SUB + k + 1, :])
                for q in range(d, chunks):
                    total[q] = total[q] + factor * moved[q - d]
        for q in range(chunks):
            near[q * SUB : (q + 1) * SUB, mine] = total[q]
        return carry

    lax.fori_loop(0, groups, group, 0)


def owner_body(lengths, arrived, owned, back, turn, stage, out, *, tokens, modes):
    blocks = arrived.shape[0]
    groups = owned.shape[0] // (modes + 2 * TAPS)
    states = modes * groups
    for c in range(stage.shape[0] // LANES):
        stage[c * LANES : (c + 1) * LANES, :] = arrived[:, c * LANES : (c + 1) * LANES].astype(jnp.float32).T
    lane = rows_of((groups, blocks), 1)

    def part(k, r):
        at = states + (k * HEAD + r) * groups
        return stage[at : at + groups, :]

    def before(k, r):
        return jnp.where(lane >= 1, pltpu.roll(part(k, r), 1, 1), 0.0)

    reach = []
    for r in range(HEAD):
        position = lane * tokens + r
        reach.append(position - doc_start(lengths, position))
    heads = []
    for k in range(2):
        ext = [before(k, r) for r in range(HEAD)] + [part(2 + k, r) for r in range(HEAD)]
        found = []
        for r in range(HEAD):
            total = jnp.zeros((groups, blocks), jnp.float32)
            for i in range(TAPS):
                at = states + (k * TAPS + i) * groups
                term = owned[at : at + groups, :] * ext[HEAD + r - i]
                total = total + jnp.where(reach[r] >= i, term, 0.0)
            found.append(total.astype(jnp.bfloat16).astype(jnp.float32))
        heads.append(found)
    products = [(a * b).astype(jnp.bfloat16).astype(jnp.float32) for a, b in zip(*heads)]
    lane = rows_of((modes, blocks), 1)
    for j in range(groups):
        at = slice(j * modes, (j + 1) * modes)
        rate = owned[at, :]
        ratio = jnp.exp(-rate)
        head = spread(products[0][j : j + 1], modes)
        for r in range(1, HEAD):
            head = head * ratio + spread(products[r][j : j + 1], modes)
        total = stage[at, :] + jnp.exp(-rate * (tokens - HEAD)) * head
        decline = jnp.exp(-rate * tokens)
        distance = 1
        while distance < blocks:
            shifted = jnp.where(lane >= distance, pltpu.roll(total, distance, 1), 0.0)
            total = total + decline * shifted
            decline = decline * decline
            distance *= 2
        out[at, :] = jnp.where(lane >= 1, pltpu.roll(total, 1, 1), 0.0)
    for c in range(states // LANES):
        back[:, c * LANES : (c + 1) * LANES] = out[c * LANES : (c + 1) * LANES, :].T.astype(jnp.bfloat16)
    turn[...] = jnp.zeros(turn.shape, jnp.float32)


def join_body(back, near, gate, top, decay, residue, gated, energy, stage):
    tokens, channels = near.shape
    modes = decay.shape[0]
    groups = channels // LANES
    chunks = tokens // SUB
    for c in range(stage.shape[0] // LANES):
        stage[c * LANES : (c + 1) * LANES, :] = back[:, c * LANES : (c + 1) * LANES].astype(jnp.float32).T
    inside = rows_of((SUB, LANES))
    odd, pair, quad = ((inside & bit) != 0 for bit in (1, 2, 4))
    squares = [jnp.zeros((SUB, LANES), jnp.float32) for _ in range(chunks)]
    for j in range(groups):
        mine = slice(j * LANES, (j + 1) * LANES)
        total = [near[q * SUB : (q + 1) * SUB, mine] for q in range(chunks)]
        rates = decay[:, mine]
        tables = powers(jnp.exp(-rates))
        start = stage[j * modes : (j + 1) * modes, :] * residue[:, mine] * jnp.sqrt(2.0 * rates)
        start = start * tables[0]
        for m in range(modes):
            one, two, four, eight = (spread(t[m : m + 1]) for t in tables)
            wave = spread(start[m : m + 1])
            wave = jnp.where(odd, wave * one, wave)
            wave = jnp.where(pair, wave * two, wave)
            wave = jnp.where(quad, wave * four, wave)
            for q in range(chunks):
                total[q] = total[q] + wave
                if q + 1 < chunks:
                    wave = wave * eight
        gates = gate[:, mine].astype(jnp.float32)
        for q in range(chunks):
            g = gates[q * SUB : (q + 1) * SUB] if q else top[:, mine]
            value = g * total[q].astype(jnp.bfloat16).astype(jnp.float32)
            gated[q * SUB : (q + 1) * SUB, mine] = value
            squares[q] = squares[q] + value * value
    summed = jnp.sum(jnp.concatenate(squares, axis=0), axis=1, keepdims=True)
    energy[...] = jnp.broadcast_to(summed, (tokens, LANES)).T[0:1, :]


def scale_body(energy, gated, gain, mixed, *, width):
    tokens, channels = gated.shape
    scaling = lax.rsqrt(jnp.sum(energy[...], axis=0, keepdims=True) / width + 1e-06)
    scaling = jnp.broadcast_to(scaling, (LANES, tokens)).T
    for j in range(channels // LANES):
        mine = slice(j * LANES, (j + 1) * LANES)
        mixed[:, mine] = (gated[:, mine] * scaling * gain[:, mine]).astype(jnp.bfloat16)


def exchange(block):
    blocks, width = block.shape
    moved = lax.all_to_all(
        block.reshape(blocks, 2, width // 2), ("gr", "gc"), split_axis=0, concat_axis=0, tiled=True
    )
    return moved.reshape(blocks, width)


def padded(rows):
    return -(-rows // (2 * LANES)) * 2 * LANES


def kernel(body, name, kinds, outs, scratch, flops, moved, given="vvvv"):
    spaces = {"s": pltpu.SMEM, "v": pltpu.VMEM, "h": pltpu.HBM}
    return pl.pallas_call(
        body,
        out_shape=outs,
        in_specs=[pl.BlockSpec(memory_space=spaces[k]) for k in kinds],
        out_specs=tuple(pl.BlockSpec(memory_space=spaces[k]) for k, _ in zip(given, outs)),
        scratch_shapes=scratch,
        compiler_params=pltpu.CompilerParams(vmem_limit_bytes=VMEM_LIMIT),
        cost_estimate=pl.CostEstimate(flops=flops, bytes_accessed=moved, transcendentals=0),
        name=name,
    )


def per_device(features, short_taps, decay, residue, doc_lengths, gain):
    _, tokens, channels = features.shape
    modes = decay.shape[0]
    blocks = lax.axis_size(("gr", "gc"))
    groups = channels // LANES
    states = groups * modes
    here = lax.axis_index(("gr", "gc")).astype(jnp.int32).reshape(1)
    f32, bf16 = jnp.float32, jnp.bfloat16
    sds = jax.ShapeDtypeStruct
    vmem = pltpu.VMEM
    out_rows = padded(states + 4 * HEAD * groups)
    wide = 2 * LANES
    front = kernel(
        front_body,
        "front",
        "hshhh",
        (sds((blocks, out_rows), bf16), sds((tokens, channels), bf16)),
        [
            vmem((out_rows, LANES), f32),
            vmem((2, tokens, channels), bf16),
            vmem(short_taps.shape, f32),
            vmem(decay.shape, f32),
            vmem((tokens, channels), bf16),
            vmem((HEAD * tokens, tokens), bf16),
            pltpu.SMEM(doc_lengths.shape, jnp.int32),
            pltpu.SemaphoreType.DMA((3 + 3 * (channels // wide),)),
        ],
        10**7,
        4 * 10**6,
        "vh",
    )
    far = functools.partial(pltpu.with_memory_space_constraint, memory_space=pltpu.HBM)
    msg, prod = front(far(doc_lengths), here, far(features), far(short_taps), far(decay))
    arrived = exchange(msg)
    gating = kernel(
        gate_body,
        "gate",
        "sshvvv",
        (
            sds((tokens, channels), bf16),
            sds((3, SUB, channels), bf16),
            sds((states + 2 * TAPS * groups, LANES), f32),
        ),
        [
            vmem(features.shape, bf16),
            vmem((HEAD * tokens, tokens), bf16),
            pltpu.SemaphoreType.DMA((3,)),
        ],
        5 * 10**7,
        4 * 10**6,
    )
    gate, ends, owned = gating(doc_lengths, here, far(features), short_taps, decay, residue)
    halo = lax.ppermute(ends, ("gr", "gc"), [(i, i + 1) for i in range(blocks - 1)])
    owner = kernel(
        functools.partial(owner_body, tokens=tokens, modes=modes),
        "owner",
        "svv",
        (sds((blocks, states), bf16), sds((SUB, LANES), f32)),
        [vmem((out_rows, LANES), f32), vmem((states, LANES), f32)],
        10**6,
        10**6,
    )
    back, turn = owner(doc_lengths, arrived, owned)
    given = exchange(back)
    local = kernel(
        near_body,
        "near",
        "ssvvhhvvv",
        (sds((tokens, channels), f32), sds((SUB, channels), f32)),
        [
            vmem((tokens, LANES), f32),
            vmem((tokens, channels), bf16),
            vmem((3, 2 * SUB, channels), bf16),
            vmem((3, SUB, channels), f32),
            pltpu.SemaphoreType.DMA((4,)),
        ],
        10**8,
        8 * 10**6,
    )
    near, top = local(doc_lengths, here, turn, halo, far(features), far(prod), short_taps, decay, residue)
    join = kernel(
        join_body,
        "join",
        "vvvvvv",
        (sds((tokens, channels), f32), sds((1, tokens), f32)),
        [vmem((states, LANES), f32)],
        10**7,
        5 * 10**6,
    )
    gated, energy = join(given, near, gate, top, decay, residue)
    energy = lax.all_gather(energy, "ch", tiled=True)
    scale = kernel(
        functools.partial(scale_body, width=float(channels * lax.axis_size("ch"))),
        "scale",
        "vvv",
        (sds((tokens, channels), bf16),),
        [],
        10**6,
        2 * 10**6,
    )
    return scale(energy, gated, gain.reshape(1, channels))[0]


def solution(mesh):
    placed = (
        P(None, ("gr", "gc"), "ch"),
        P(None, None, "ch"),
        P(None, "ch"),
        P(None, "ch"),
        P(),
        P("ch"),
    )
    return jax.shard_map(
        per_device, mesh=mesh, in_specs=placed, out_specs=P(("gr", "gc"), "ch"), check_vma=False
    )
```

```python
import functools

import jax
import jax.numpy as jnp
from jax import lax
from jax.experimental import pallas as pl
from jax.experimental.pallas import tpu as pltpu
from jax.sharding import PartitionSpec as P


LANES = 128
TAPS = 7
HEAD = TAPS - 1
SUB = 8
VMEM_LIMIT = 12 * 1024 * 1024


def doc_start(lengths, position):
    start, found = jnp.int32(0), jnp.zeros_like(position)
    for doc in range(lengths.shape[0]):
        found = jnp.where(position >= start, jnp.maximum(found, start), found)
        start = start + lengths[doc]
    return found


def short_conv(shifts, x, taps):
    tokens = x.shape[0]
    moved = jnp.dot(shifts, x, preferred_element_type=jnp.float32)
    total = x.astype(jnp.float32) * taps(0)
    for i in range(1, TAPS):
        total = total + moved[(i - 1) * tokens : i * tokens] * taps(i)
    return total.astype(jnp.bfloat16)


def rows_of(shape, dim=0):
    return lax.broadcasted_iota(jnp.int32, shape, dim)


def powers(ratio):
    square = ratio * ratio
    fourth = square * square
    return ratio, square, fourth, fourth * fourth


def spread(row, rows=SUB):
    return jnp.broadcast_to(row, (rows, row.shape[1]))


def fill_shifts(shifts, lengths, first_token):
    tokens = shifts.shape[1]
    row = rows_of((tokens, tokens))
    column = rows_of((tokens, tokens), 1)
    position = row + first_token
    reach = position - doc_start(lengths, position)
    for i in range(1, TAPS):
        hit = (column == row - i) & (reach >= i)
        shifts[(i - 1) * tokens : i * tokens, :] = jnp.where(hit, 1.0, 0.0).astype(jnp.bfloat16)


def product_of(shifts, feats, taps):
    first, third = (short_conv(shifts, f, t) for f, t in zip(feats, taps))
    product = first.astype(jnp.float32) * third.astype(jnp.float32)
    inside = rows_of(product.shape) >= HEAD
    return jnp.where(inside, product, 0.0).astype(jnp.bfloat16)


def front_body(lengths_hbm, here, feats_hbm, taps_hbm, decay_hbm, msg, stage, feats, tail, taps, decay, shifts, lengths, sems):
    pair, tokens, channels = feats.shape
    modes = decay.shape[0]
    groups = channels // LANES
    counted = pltpu.make_async_copy(lengths_hbm, lengths, sems.at[0])
    others = [
        pltpu.make_async_copy(feats_hbm.at[2 * k], feats.at[k], sems.at[1 + k]) for k in range(pair)
    ] + [
        pltpu.make_async_copy(taps_hbm, taps, sems.at[3]),
        pltpu.make_async_copy(decay_hbm, decay, sems.at[4]),
        pltpu.make_async_copy(feats_hbm.at[1, tokens - 2 * SUB : tokens, :], tail, sems.at[5]),
    ]
    counted.start()
    for copy in others:
        copy.start()
    states = groups * modes
    used = states + 5 * HEAD * groups
    if used < stage.shape[0]:
        stage[used:, :] = jnp.zeros((stage.shape[0] - used, LANES), jnp.float32)
    counted.wait()
    fill_shifts(shifts, lengths, here[0] * tokens)
    for copy in others:
        copy.wait()
    values = product_of(
        shifts[...],
        [feats[k] for k in range(pair)],
        [lambda i, k=k: taps[2 * k, i : i + 1, :] for k in range(pair)],
    ).astype(jnp.float32)
    for j in range(groups):
        mine = slice(j * LANES, (j + 1) * LANES)
        v = values[:, mine]
        tables = powers(jnp.exp(-decay[:, mine]))
        for m in range(modes):
            one, two, four, eight = (spread(t[m : m + 1]) for t in tables)
            state = v[0:SUB]
            for q in range(1, tokens // SUB):
                state = state * eight + v[q * SUB : (q + 1) * SUB]
            state = state * four + pltpu.roll(state, SUB - 4, 0)
            state = state * two + pltpu.roll(state, SUB - 2, 0)
            state = state * one + pltpu.roll(state, SUB - 1, 0)
            stage[j * modes + m : j * modes + m + 1, :] = state[0:1]
        at = states
        last = slice(tokens - 2 * SUB, tokens)
        for part, skip in (
            (feats[0, last, mine], 2 * SUB - HEAD),
            (feats[1, last, mine], 2 * SUB - HEAD),
            (tail[:, mine], 2 * SUB - HEAD),
            (feats[0, 0 : 2 * SUB, mine], 0),
            (feats[1, 0 : 2 * SUB, mine], 0),
        ):
            part = part.astype(jnp.float32)
            for r in range(HEAD):
                stage[at + r * groups + j : at + r * groups + j + 1, :] = part[skip + r : skip + r + 1]
            at += HEAD * groups
    for c in range(stage.shape[0] // LANES):
        msg[:, c * LANES : (c + 1) * LANES] = stage[c * LANES : (c + 1) * LANES, :].T.astype(jnp.bfloat16)


def local_body(
    lengths, here, feats_hbm, taps, decay, residue, gate, near, edge, owned, table, feats, prod, shifts, sems
):
    _, tokens, channels = feats.shape
    modes = decay.shape[0]
    copies = [pltpu.make_async_copy(feats_hbm.at[b], feats.at[b], sems.at[b]) for b in range(3)]
    for copy in copies:
        copy.start()
    fill_shifts(shifts, lengths, here[0] * tokens)
    for copy in copies:
        copy.wait()
    groups = channels // LANES
    chunks = tokens // SUB
    wide = 4 * LANES
    for block in range(channels // wide):
        lanes = slice(block * wide, (block + 1) * wide)
        gate[:, lanes] = short_conv(shifts[...], feats[1, :, lanes], lambda i: taps[1, i : i + 1, lanes])
        prod[:, lanes] = product_of(
            shifts[...],
            [feats[b, :, lanes] for b in (0, 2)],
            [lambda i, b=b: taps[b, i : i + 1, lanes] for b in (0, 2)],
        )
    states = groups * modes
    edge[...] = feats[1, 0 : 2 * SUB, :].astype(jnp.float32)[0:SUB]
    chosen = rows_of((modes, LANES), 1) == here[0]
    chosen_taps = rows_of((TAPS, LANES), 1) == here[0]
    for j in range(groups):
        mine = slice(j * LANES, (j + 1) * LANES)
        at = slice(j * modes, (j + 1) * modes)
        rates, scale = decay[:, mine], residue[:, mine]
        scale = scale * jnp.sqrt(2.0 * rates)
        pick = jnp.sum(jnp.where(chosen, rates, 0.0), axis=1, keepdims=True)
        owned[at, :] = jnp.broadcast_to(pick, (modes, LANES))
        pick = jnp.sum(jnp.where(chosen, scale, 0.0), axis=1, keepdims=True)
        owned[states + j * modes : states + (j + 1) * modes, :] = jnp.broadcast_to(pick, (modes, LANES))
        for b in range(3):
            pick = jnp.sum(jnp.where(chosen_taps, taps[b, :, mine], 0.0), axis=1, keepdims=True)
            pick = jnp.broadcast_to(pick, (TAPS, LANES))
            for i in range(TAPS):
                to = 2 * states + (b * TAPS + i) * groups + j
                owned[to : to + 1, :] = pick[i : i + 1]
    inside = rows_of((SUB, LANES))
    steps = inside.astype(jnp.float32)

    def group(j, carry):
        mine = pl.ds(pl.multiple_of(j * LANES, LANES), LANES)
        sums = [jnp.zeros((SUB, LANES), jnp.float32) for _ in range(chunks)]
        rates = decay[:, mine]
        weights = residue[:, mine] * jnp.sqrt(2.0 * rates)
        eights = jnp.exp(-SUB * rates)
        for m in range(modes):
            step = spread(eights[m : m + 1])
            wave = weights[m : m + 1] * jnp.exp(-rates[m : m + 1] * steps)
            for q in range(chunks):
                sums[q] = sums[q] + wave
                if q + 1 < chunks:
                    wave = wave * step
        for q in range(chunks):
            table[q * SUB : (q + 1) * SUB, :] = sums[q]
        values = prod[:, mine].astype(jnp.float32)
        total = [jnp.zeros((SUB, LANES), jnp.float32) for _ in range(chunks)]
        for k in range(SUB):
            if k:
                turned = [
                    pltpu.roll(values[q * SUB : (q + 1) * SUB], k, 0) for q in range(chunks)
                ]
                low = inside < k
                moved = [
                    jnp.where(low, turned[q - 1] if q else 0.0, turned[q]) for q in range(chunks)
                ]
            else:
                moved = [values[q * SUB : (q + 1) * SUB] for q in range(chunks)]
            for d in range(chunks):
                factor = jnp.broadcast_to(table[d * SUB + k : d * SUB + k + 1, :], (SUB, LANES))
                for q in range(d, chunks):
                    total[q] = total[q] + factor * moved[q - d]
        for q in range(chunks):
            near[q * SUB : (q + 1) * SUB, mine] = total[q]
        return carry

    lax.fori_loop(0, groups, group, 0)


def owner_body(lengths, arrived, owned, back, stage, out, *, tokens, modes):
    blocks = arrived.shape[0]
    groups = owned.shape[0] // (2 * modes + 3 * TAPS)
    states = modes * groups
    for c in range(stage.shape[0] // LANES):
        stage[c * LANES : (c + 1) * LANES, :] = arrived[:, c * LANES : (c + 1) * LANES].astype(jnp.float32).T
    lane = rows_of((groups, blocks), 1)

    def part(k, r):
        at = states + (k * HEAD + r) * groups
        return stage[at : at + groups, :]

    def before(k, r):
        return jnp.where(lane >= 1, pltpu.roll(part(k, r), 1, 1), 0.0)

    reach = []
    for r in range(HEAD):
        position = lane * tokens + r
        reach.append(position - doc_start(lengths, position))
    heads = []
    for last, first, b in ((0, 3, 0), (1, 4, 2)):
        ext = [before(last, r) for r in range(HEAD)] + [part(first, r) for r in range(HEAD)]
        found = []
        for r in range(HEAD):
            total = jnp.zeros((groups, blocks), jnp.float32)
            for i in range(TAPS):
                at = 2 * states + (b * TAPS + i) * groups
                term = owned[at : at + groups, :] * ext[HEAD + r - i]
                total = total + jnp.where(reach[r] >= i, term, 0.0)
            found.append(total.astype(jnp.bfloat16).astype(jnp.float32))
        heads.append(found)
    products = [(a * b).astype(jnp.bfloat16).astype(jnp.float32) for a, b in zip(*heads)]
    lane = rows_of((modes, blocks), 1)
    for j in range(groups):
        at = slice(j * modes, (j + 1) * modes)
        rate, weight = owned[at, :], owned[states + j * modes : states + (j + 1) * modes, :]
        ratio = jnp.exp(-rate)
        rows = [spread(p[j : j + 1], modes) for p in products]
        head = rows[0]
        for r in range(1, HEAD):
            head = head * ratio + rows[r]
        total = stage[at, :] + jnp.exp(-rate * (tokens - HEAD)) * head
        decline = jnp.exp(-rate * tokens)
        distance = 1
        while distance < blocks:
            shifted = jnp.where(lane >= distance, pltpu.roll(total, distance, 1), 0.0)
            total = total + decline * shifted
            decline = decline * decline
            distance *= 2
        state = jnp.where(lane >= 1, pltpu.roll(total, 1, 1), 0.0)
        for r in range(HEAD):
            state = state * ratio + rows[r]
            to = states + r * groups + j
            out[to : to + 1, :] = jnp.sum(state * weight, axis=0, keepdims=True)
        out[at, :] = state
    at = states + HEAD * groups
    for r in range(HEAD):
        out[at + r * groups : at + (r + 1) * groups, :] = before(2, r)
    used = states + 2 * HEAD * groups
    if used < out.shape[0]:
        out[used:, :] = jnp.zeros((out.shape[0] - used, LANES), jnp.float32)
    for c in range(out.shape[0] // LANES):
        back[:, c * LANES : (c + 1) * LANES] = out[c * LANES : (c + 1) * LANES, :].T.astype(jnp.bfloat16)


def join_body(lengths, here, back, near, gate, edge, decay, residue, taps, gated, energy, stage):
    tokens, channels = near.shape
    modes = decay.shape[0]
    groups = channels // LANES
    chunks = tokens // SUB
    states = groups * modes
    for c in range(stage.shape[0] // LANES):
        stage[c * LANES : (c + 1) * LANES, :] = back[:, c * LANES : (c + 1) * LANES].astype(jnp.float32).T
    inside = rows_of((SUB, LANES))
    position = inside + here[0] * tokens
    reach = position - doc_start(lengths, position)
    odd, pair, quad = ((inside & bit) != 0 for bit in (1, 2, 4))
    squares = [jnp.zeros((SUB, LANES), jnp.float32) for _ in range(chunks)]
    for j in range(groups):
        mine = slice(j * LANES, (j + 1) * LANES)
        total = [near[q * SUB : (q + 1) * SUB, mine] for q in range(chunks)]
        rates = decay[:, mine]
        tables = powers(jnp.exp(-rates))
        start = stage[j * modes : (j + 1) * modes, :] * residue[:, mine] * jnp.sqrt(2.0 * rates)
        start = start * tables[0] * tables[1]
        grown = jnp.exp(SUB * rates)
        for m in range(modes):
            one, two, four, eight = (spread(t[m : m + 1]) for t in tables)
            wave = spread(start[m : m + 1])
            wave = jnp.where(odd, wave * one, wave)
            wave = jnp.where(pair, wave * two, wave)
            wave = jnp.where(quad, wave * four, wave)
            total[0] = total[0] + wave * spread(grown[m : m + 1])
            for q in range(1, chunks):
                total[q] = total[q] + wave
                if q + 1 < chunks:
                    wave = wave * eight
        at = states + j
        pieces = [stage[at + r * groups : at + r * groups + 1, :] for r in range(HEAD)]
        total[0] = jnp.concatenate(pieces + [total[0][HEAD:SUB]], axis=0)
        at += HEAD * groups
        pieces = [stage[at + r * groups : at + r * groups + 1, :] for r in range(HEAD)]
        ext = jnp.concatenate(pieces + [edge[:, mine], jnp.zeros((2, LANES), jnp.float32)], axis=0)
        front = jnp.zeros((SUB, LANES), jnp.float32)
        for i in range(TAPS):
            term = taps[1, i : i + 1, mine] * ext[HEAD - i : HEAD - i + SUB]
            front = front + jnp.where(reach >= i, term, 0.0)
        front = front.astype(jnp.bfloat16).astype(jnp.float32)
        gates = gate[:, mine].astype(jnp.float32)
        for q in range(chunks):
            g = gates[q * SUB : (q + 1) * SUB] if q else front
            value = g * total[q].astype(jnp.bfloat16).astype(jnp.float32)
            gated[q * SUB : (q + 1) * SUB, mine] = value
            squares[q] = squares[q] + value * value
    summed = jnp.sum(jnp.concatenate(squares, axis=0), axis=1, keepdims=True)
    energy[...] = jnp.broadcast_to(summed, (tokens, LANES)).T[0:1, :]


def scale_body(energy, gated, gain, mixed, *, width):
    tokens, channels = gated.shape
    scaling = lax.rsqrt(jnp.sum(energy[...], axis=0, keepdims=True) / width + 1e-06)
    scaling = jnp.broadcast_to(scaling, (LANES, tokens)).T
    for j in range(channels // LANES):
        mine = slice(j * LANES, (j + 1) * LANES)
        mixed[:, mine] = (gated[:, mine] * scaling * gain[:, mine]).astype(jnp.bfloat16)


def exchange(block):
    blocks, width = block.shape
    moved = lax.all_to_all(
        block.reshape(blocks, 2, width // 2), ("gr", "gc"), split_axis=0, concat_axis=0, tiled=True
    )
    return moved.reshape(blocks, width)


def padded(rows):
    return -(-rows // (2 * LANES)) * 2 * LANES


def kernel(body, name, kinds, outs, scratch, flops, moved):
    spaces = {"s": pltpu.SMEM, "v": pltpu.VMEM, "h": pltpu.HBM}
    return pl.pallas_call(
        body,
        out_shape=outs,
        in_specs=[pl.BlockSpec(memory_space=spaces[k]) for k in kinds],
        out_specs=tuple(pl.BlockSpec(memory_space=pltpu.VMEM) for _ in outs),
        scratch_shapes=scratch,
        compiler_params=pltpu.CompilerParams(vmem_limit_bytes=VMEM_LIMIT),
        cost_estimate=pl.CostEstimate(flops=flops, bytes_accessed=moved, transcendentals=0),
        name=name,
    )


def per_device(features, short_taps, decay, residue, doc_lengths, gain):
    _, tokens, channels = features.shape
    modes = decay.shape[0]
    blocks = lax.axis_size(("gr", "gc"))
    groups = channels // LANES
    states = groups * modes
    here = lax.axis_index(("gr", "gc")).astype(jnp.int32).reshape(1)
    f32, bf16 = jnp.float32, jnp.bfloat16
    sds = jax.ShapeDtypeStruct
    vmem = pltpu.VMEM
    out_rows = padded(states + 5 * HEAD * groups)
    back_rows = padded(states + 2 * HEAD * groups)
    front = kernel(
        front_body,
        "front",
        "hshhh",
        (sds((blocks, out_rows), bf16),),
        [
            vmem((out_rows, LANES), f32),
            vmem((2, tokens, channels), bf16),
            vmem((2 * SUB, channels), bf16),
            vmem(short_taps.shape, f32),
            vmem(decay.shape, f32),
            vmem((HEAD * tokens, tokens), bf16),
            pltpu.SMEM(doc_lengths.shape, jnp.int32),
            pltpu.SemaphoreType.DMA((6,)),
        ],
        10**7,
        4 * 10**6,
    )
    far = functools.partial(pltpu.with_memory_space_constraint, memory_space=pltpu.HBM)
    msg = front(far(doc_lengths), here, far(features), far(short_taps), far(decay))[0]
    arrived = exchange(msg)
    local = kernel(
        local_body,
        "local",
        "sshvvv",
        (
            sds((tokens, channels), bf16),
            sds((tokens, channels), f32),
            sds((SUB, channels), f32),
            sds((2 * states + 3 * TAPS * groups, LANES), f32),
        ),
        [
            vmem((tokens, LANES), f32),
            vmem(features.shape, bf16),
            vmem((tokens, channels), bf16),
            vmem((HEAD * tokens, tokens), bf16),
            pltpu.SemaphoreType.DMA((3,)),
        ],
        10**8,
        8 * 10**6,
    )
    gate, near, edge, owned = local(doc_lengths, here, far(features), short_taps, decay, residue)
    owner = kernel(
        functools.partial(owner_body, tokens=tokens, modes=modes),
        "owner",
        "svv",
        (sds((blocks, back_rows), bf16),),
        [vmem((out_rows, LANES), f32), vmem((back_rows, LANES), f32)],
        10**6,
        10**6,
    )
    given = exchange(owner(doc_lengths, arrived, owned)[0])
    parts = lax.axis_size("ch")
    join = kernel(
        join_body,
        "join",
        "ssvvvvvvv",
        (sds((tokens, channels), f32), sds((1, tokens), f32)),
        [vmem((back_rows, LANES), f32)],
        10**7,
        5 * 10**6,
    )
    gated, energy = join(doc_lengths, here, given, near, gate, edge, decay, residue, short_taps)
    energy = lax.all_gather(energy, "ch", tiled=True)
    scale = kernel(
        functools.partial(scale_body, width=float(channels * parts)),
        "scale",
        "vvv",
        (sds((tokens, channels), bf16),),
        [],
        10**6,
        2 * 10**6,
    )
    return scale(energy, gated, gain.reshape(1, channels))[0]


def solution(mesh):
    placed = (
        P(None, ("gr", "gc"), "ch"),
        P(None, None, "ch"),
        P(None, "ch"),
        P(None, "ch"),
        P(),
        P("ch"),
    )
    return jax.shard_map(
        per_device, mesh=mesh, in_specs=placed, out_specs=P(("gr", "gc"), "ch"), check_vma=False
    )
```

```python
import functools

import jax
import jax.numpy as jnp
from jax import lax
from jax.experimental import pallas as pl
from jax.experimental.pallas import tpu as pltpu
from jax.sharding import PartitionSpec as P


LANES = 128
TAPS = 7
HEAD = TAPS - 1
SUB = 8
VMEM_LIMIT = 12 * 1024 * 1024


def doc_start(lengths, position):
    start, found = jnp.int32(0), jnp.zeros_like(position)
    for doc in range(lengths.shape[0]):
        found = jnp.where(position >= start, jnp.maximum(found, start), found)
        start = start + lengths[doc]
    return found


def short_conv(shifts, x, taps):
    tokens = x.shape[0]
    moved = jnp.dot(shifts, x, preferred_element_type=jnp.float32)
    total = x.astype(jnp.float32) * taps(0)
    for i in range(1, TAPS):
        total = total + moved[(i - 1) * tokens : i * tokens] * taps(i)
    return total.astype(jnp.bfloat16)


def rows_of(shape, dim=0):
    return lax.broadcasted_iota(jnp.int32, shape, dim)


def powers(ratio):
    square = ratio * ratio
    fourth = square * square
    return ratio, square, fourth, fourth * fourth


def spread(row, rows=SUB):
    return jnp.broadcast_to(row, (rows, row.shape[1]))


def fill_shifts(shifts, lengths, first_token):
    tokens = shifts.shape[1]
    row = rows_of((tokens, tokens))
    column = rows_of((tokens, tokens), 1)
    position = row + first_token
    reach = position - doc_start(lengths, position)
    for i in range(1, TAPS):
        hit = (column == row - i) & (reach >= i)
        shifts[(i - 1) * tokens : i * tokens, :] = jnp.where(hit, 1.0, 0.0).astype(jnp.bfloat16)


def product_of(first, third):
    product = first.astype(jnp.float32) * third.astype(jnp.float32)
    return jnp.where(rows_of(product.shape) >= HEAD, product, 0.0).astype(jnp.bfloat16)


def front_body(lengths_hbm, here, feats_hbm, taps_hbm, decay_hbm, msg, stage, feats, tail, taps, decay, shifts, lengths, sems):
    pair, tokens, channels = feats.shape
    modes = decay.shape[0]
    groups = channels // LANES
    counted = pltpu.make_async_copy(lengths_hbm, lengths, sems.at[0])
    branches = [pltpu.make_async_copy(feats_hbm.at[2 * k], feats.at[k], sems.at[1 + k]) for k in range(pair)]
    tapped = pltpu.make_async_copy(taps_hbm, taps, sems.at[3])
    others = (
        pltpu.make_async_copy(decay_hbm, decay, sems.at[4]),
        pltpu.make_async_copy(feats_hbm.at[1, tokens - 2 * SUB : tokens, :], tail, sems.at[5]),
    )
    counted.start()
    branches[0].start()
    tapped.start()
    branches[1].start()
    for copy in others:
        copy.start()
    states = groups * modes
    used = states + 5 * HEAD * groups
    if used < stage.shape[0]:
        stage[used:, :] = jnp.zeros((stage.shape[0] - used, LANES), jnp.float32)
    counted.wait()
    fill_shifts(shifts, lengths, here[0] * tokens)
    tapped.wait()
    found = []
    for k in range(pair):
        branches[k].wait()
        found.append(short_conv(shifts[...], feats[k], lambda i, k=k: taps[2 * k, i : i + 1, :]))
    values = product_of(*found).astype(jnp.float32)
    for copy in others:
        copy.wait()
    for j in range(groups):
        mine = slice(j * LANES, (j + 1) * LANES)
        v = values[:, mine]
        tables = powers(jnp.exp(-decay[:, mine]))
        for m in range(modes):
            one, two, four, eight = (spread(t[m : m + 1]) for t in tables)
            state = v[0:SUB]
            for q in range(1, tokens // SUB):
                state = state * eight + v[q * SUB : (q + 1) * SUB]
            state = state * four + pltpu.roll(state, SUB - 4, 0)
            state = state * two + pltpu.roll(state, SUB - 2, 0)
            state = state * one + pltpu.roll(state, SUB - 1, 0)
            stage[j * modes + m : j * modes + m + 1, :] = state[0:1]
        at = states
        last = slice(tokens - 2 * SUB, tokens)
        for part, skip in (
            (feats[0, last, mine], 2 * SUB - HEAD),
            (feats[1, last, mine], 2 * SUB - HEAD),
            (tail[:, mine], 2 * SUB - HEAD),
            (feats[0, 0 : 2 * SUB, mine], 0),
            (feats[1, 0 : 2 * SUB, mine], 0),
        ):
            part = part.astype(jnp.float32)
            for r in range(HEAD):
                stage[at + r * groups + j : at + r * groups + j + 1, :] = part[skip + r : skip + r + 1]
            at += HEAD * groups
    for c in range(stage.shape[0] // LANES):
        msg[:, c * LANES : (c + 1) * LANES] = stage[c * LANES : (c + 1) * LANES, :].T.astype(jnp.bfloat16)


def local_body(
    lengths, here, feats_hbm, taps, decay, residue, gate, near, edge, owned, table, feats, prod, shifts, sems
):
    _, tokens, channels = feats.shape
    modes = decay.shape[0]
    copies = [pltpu.make_async_copy(feats_hbm.at[b], feats.at[b], sems.at[b]) for b in range(3)]
    for copy in copies:
        copy.start()
    fill_shifts(shifts, lengths, here[0] * tokens)
    for copy in copies:
        copy.wait()
    groups = channels // LANES
    chunks = tokens // SUB
    wide = 4 * LANES
    for block in range(channels // wide):
        lanes = slice(block * wide, (block + 1) * wide)
        gate[:, lanes] = short_conv(shifts[...], feats[1, :, lanes], lambda i: taps[1, i : i + 1, lanes])
        prod[:, lanes] = product_of(
            *(
                short_conv(shifts[...], feats[b, :, lanes], lambda i, b=b: taps[b, i : i + 1, lanes])
                for b in (0, 2)
            )
        )
    states = groups * modes
    edge[...] = feats[1, 0 : 2 * SUB, :].astype(jnp.float32)[0:SUB]
    chosen = rows_of((modes, LANES), 1) == here[0]
    chosen_taps = rows_of((TAPS, LANES), 1) == here[0]
    for j in range(groups):
        mine = slice(j * LANES, (j + 1) * LANES)
        rates, scale = decay[:, mine], residue[:, mine]
        scale = scale * jnp.sqrt(2.0 * rates)
        pick = jnp.sum(jnp.where(chosen, rates, 0.0), axis=1, keepdims=True)
        pick = jnp.broadcast_to(pick, (modes, LANES))
        for k, count in enumerate((1, tokens - HEAD, tokens)):
            to = k * states + j * modes
            owned[to : to + modes, :] = jnp.exp(-pick * count)
        pick = jnp.sum(jnp.where(chosen, scale, 0.0), axis=1, keepdims=True)
        to = 3 * states + j * modes
        owned[to : to + modes, :] = jnp.broadcast_to(pick, (modes, LANES))
        for b in range(3):
            pick = jnp.sum(jnp.where(chosen_taps, taps[b, :, mine], 0.0), axis=1, keepdims=True)
            pick = jnp.broadcast_to(pick, (TAPS, LANES))
            for i in range(TAPS):
                to = 4 * states + (b * TAPS + i) * groups + j
                owned[to : to + 1, :] = pick[i : i + 1]
    inside = rows_of((SUB, LANES))
    steps = inside.astype(jnp.float32)

    def group(j, carry):
        mine = pl.ds(pl.multiple_of(j * LANES, LANES), LANES)
        sums = [jnp.zeros((SUB, LANES), jnp.float32) for _ in range(chunks)]
        rates = decay[:, mine]
        weights = residue[:, mine] * jnp.sqrt(2.0 * rates)
        eights = jnp.exp(-SUB * rates)
        for m in range(modes):
            step = spread(eights[m : m + 1])
            wave = weights[m : m + 1] * jnp.exp(-rates[m : m + 1] * steps)
            for q in range(chunks):
                sums[q] = sums[q] + wave
                if q + 1 < chunks:
                    wave = wave * step
        for q in range(chunks):
            table[q * SUB : (q + 1) * SUB, :] = sums[q]
        values = prod[:, mine].astype(jnp.float32)
        total = [jnp.zeros((SUB, LANES), jnp.float32) for _ in range(chunks)]
        for k in range(SUB):
            if k:
                turned = [
                    pltpu.roll(values[q * SUB : (q + 1) * SUB], k, 0) for q in range(chunks)
                ]
                low = inside < k
                moved = [
                    jnp.where(low, turned[q - 1] if q else 0.0, turned[q]) for q in range(chunks)
                ]
            else:
                moved = [values[q * SUB : (q + 1) * SUB] for q in range(chunks)]
            for d in range(chunks):
                factor = jnp.broadcast_to(table[d * SUB + k : d * SUB + k + 1, :], (SUB, LANES))
                for q in range(d, chunks):
                    total[q] = total[q] + factor * moved[q - d]
        for q in range(chunks):
            near[q * SUB : (q + 1) * SUB, mine] = total[q]
        return carry

    lax.fori_loop(0, groups, group, 0)


def owner_body(lengths, arrived, owned, back, stage, out, *, tokens, modes):
    blocks = arrived.shape[0]
    groups = owned.shape[0] // (4 * modes + 3 * TAPS)
    states = modes * groups
    for c in range(stage.shape[0] // LANES):
        stage[c * LANES : (c + 1) * LANES, :] = arrived[:, c * LANES : (c + 1) * LANES].astype(jnp.float32).T
    lane = rows_of((groups, blocks), 1)

    def part(k, r):
        at = states + (k * HEAD + r) * groups
        return stage[at : at + groups, :]

    def before(k, r):
        return jnp.where(lane >= 1, pltpu.roll(part(k, r), 1, 1), 0.0)

    reach = []
    for r in range(HEAD):
        position = lane * tokens + r
        reach.append(position - doc_start(lengths, position))
    heads = []
    for last, first, b in ((0, 3, 0), (1, 4, 2)):
        ext = [before(last, r) for r in range(HEAD)] + [part(first, r) for r in range(HEAD)]
        found = []
        for r in range(HEAD):
            total = jnp.zeros((groups, blocks), jnp.float32)
            for i in range(TAPS):
                at = 4 * states + (b * TAPS + i) * groups
                term = owned[at : at + groups, :] * ext[HEAD + r - i]
                total = total + jnp.where(reach[r] >= i, term, 0.0)
            found.append(total.astype(jnp.bfloat16).astype(jnp.float32))
        heads.append(found)
    products = [(a * b).astype(jnp.bfloat16).astype(jnp.float32) for a, b in zip(*heads)]
    lane = rows_of((modes, blocks), 1)
    for j in range(groups):
        at = slice(j * modes, (j + 1) * modes)
        ratio, distant, decline, weight = (
            owned[k * states + j * modes : k * states + (j + 1) * modes, :] for k in range(4)
        )
        rows = [spread(p[j : j + 1], modes) for p in products]
        head = rows[0]
        for r in range(1, HEAD):
            head = head * ratio + rows[r]
        total = stage[at, :] + distant * head
        distance = 1
        while distance < blocks:
            shifted = jnp.where(lane >= distance, pltpu.roll(total, distance, 1), 0.0)
            total = total + decline * shifted
            decline = decline * decline
            distance *= 2
        state = jnp.where(lane >= 1, pltpu.roll(total, 1, 1), 0.0)
        for r in range(HEAD):
            state = state * ratio + rows[r]
            to = states + r * groups + j
            out[to : to + 1, :] = jnp.sum(state * weight, axis=0, keepdims=True)
        out[at, :] = state
    at = states + HEAD * groups
    for r in range(HEAD):
        out[at + r * groups : at + (r + 1) * groups, :] = before(2, r)
    used = states + 2 * HEAD * groups
    if used < out.shape[0]:
        out[used:, :] = jnp.zeros((out.shape[0] - used, LANES), jnp.float32)
    for c in range(out.shape[0] // LANES):
        back[:, c * LANES : (c + 1) * LANES] = out[c * LANES : (c + 1) * LANES, :].T.astype(jnp.bfloat16)


def join_body(lengths, here, back, near, gate, edge, decay, residue, taps, gated, energy, stage):
    tokens, channels = near.shape
    modes = decay.shape[0]
    groups = channels // LANES
    chunks = tokens // SUB
    states = groups * modes
    for c in range(stage.shape[0] // LANES):
        stage[c * LANES : (c + 1) * LANES, :] = back[:, c * LANES : (c + 1) * LANES].astype(jnp.float32).T
    inside = rows_of((SUB, LANES))
    position = inside + here[0] * tokens
    reach = position - doc_start(lengths, position)
    odd, pair, quad = ((inside & bit) != 0 for bit in (1, 2, 4))
    squares = [jnp.zeros((SUB, LANES), jnp.float32) for _ in range(chunks)]
    for j in range(groups):
        mine = slice(j * LANES, (j + 1) * LANES)
        total = [near[q * SUB : (q + 1) * SUB, mine] for q in range(chunks)]
        rates = decay[:, mine]
        tables = powers(jnp.exp(-rates))
        start = stage[j * modes : (j + 1) * modes, :] * residue[:, mine] * jnp.sqrt(2.0 * rates)
        start = start * tables[0] * tables[1]
        grown = jnp.exp(SUB * rates)
        for m in range(modes):
            one, two, four, eight = (spread(t[m : m + 1]) for t in tables)
            wave = spread(start[m : m + 1])
            wave = jnp.where(odd, wave * one, wave)
            wave = jnp.where(pair, wave * two, wave)
            wave = jnp.where(quad, wave * four, wave)
            total[0] = total[0] + wave * spread(grown[m : m + 1])
            for q in range(1, chunks):
                total[q] = total[q] + wave
                if q + 1 < chunks:
                    wave = wave * eight
        told = stage[pl.ds(states + j, SUB, stride=groups), :]
        total[0] = jnp.where(inside < HEAD, told, total[0])
        before = stage[pl.ds(states + HEAD * groups + j, SUB, stride=groups), :]
        now = edge[:, mine]
        front = now * taps[1, 0:1, mine]
        for i in range(1, TAPS):
            moved = jnp.where(inside < i, pltpu.roll(before, (SUB - HEAD + i) % SUB, 0), pltpu.roll(now, i, 0))
            front = front + jnp.where(reach >= i, moved * taps[1, i : i + 1, mine], 0.0)
        front = front.astype(jnp.bfloat16).astype(jnp.float32)
        gates = gate[:, mine].astype(jnp.float32)
        for q in range(chunks):
            g = gates[q * SUB : (q + 1) * SUB] if q else front
            value = g * total[q].astype(jnp.bfloat16).astype(jnp.float32)
            gated[q * SUB : (q + 1) * SUB, mine] = value
            squares[q] = squares[q] + value * value
    summed = jnp.sum(jnp.concatenate(squares, axis=0), axis=1, keepdims=True)
    energy[...] = jnp.broadcast_to(summed, (tokens, LANES)).T[0:1, :]


def scale_body(energy, gated, gain, mixed_hbm, mixed, sems, *, width):
    tokens, channels = gated.shape
    pieces = sems.shape[0]
    rows = tokens // pieces
    scaling = lax.rsqrt(jnp.sum(energy[...], axis=0, keepdims=True) / width + 1e-06)
    scaling = jnp.broadcast_to(scaling, (LANES, tokens)).T
    copies = []
    for k in range(pieces):
        part = slice(k * rows, (k + 1) * rows)
        for j in range(channels // LANES):
            mine = slice(j * LANES, (j + 1) * LANES)
            mixed[part, mine] = (gated[part, mine] * scaling[part] * gain[:, mine]).astype(jnp.bfloat16)
        copies.append(pltpu.make_async_copy(mixed.at[part, :], mixed_hbm.at[part, :], sems.at[k]))
        copies[k].start()
    for copy in copies:
        copy.wait()


def exchange(block):
    blocks, width = block.shape
    moved = lax.all_to_all(
        block.reshape(blocks, 2, width // 2), ("gr", "gc"), split_axis=0, concat_axis=0, tiled=True
    )
    return moved.reshape(blocks, width)


def padded(rows):
    return -(-rows // (2 * LANES)) * 2 * LANES


def kernel(body, name, kinds, outs, scratch, flops, moved, to=pltpu.VMEM):
    spaces = {"s": pltpu.SMEM, "v": pltpu.VMEM, "h": pltpu.HBM}
    return pl.pallas_call(
        body,
        out_shape=outs,
        in_specs=[pl.BlockSpec(memory_space=spaces[k]) for k in kinds],
        out_specs=tuple(pl.BlockSpec(memory_space=to) for _ in outs),
        scratch_shapes=scratch,
        compiler_params=pltpu.CompilerParams(vmem_limit_bytes=VMEM_LIMIT),
        cost_estimate=pl.CostEstimate(flops=flops, bytes_accessed=moved, transcendentals=0),
        name=name,
    )


def per_device(features, short_taps, decay, residue, doc_lengths, gain):
    _, tokens, channels = features.shape
    modes = decay.shape[0]
    blocks = lax.axis_size(("gr", "gc"))
    groups = channels // LANES
    states = groups * modes
    here = lax.axis_index(("gr", "gc")).astype(jnp.int32).reshape(1)
    f32, bf16 = jnp.float32, jnp.bfloat16
    sds = jax.ShapeDtypeStruct
    vmem = pltpu.VMEM
    out_rows = padded(states + 5 * HEAD * groups)
    back_rows = padded(states + 2 * HEAD * groups)
    front = kernel(
        front_body,
        "front",
        "hshhh",
        (sds((blocks, out_rows), bf16),),
        [
            vmem((out_rows, LANES), f32),
            vmem((2, tokens, channels), bf16),
            vmem((2 * SUB, channels), bf16),
            vmem(short_taps.shape, f32),
            vmem(decay.shape, f32),
            vmem((HEAD * tokens, tokens), bf16),
            pltpu.SMEM(doc_lengths.shape, jnp.int32),
            pltpu.SemaphoreType.DMA((6,)),
        ],
        10**7,
        4 * 10**6,
    )
    far = functools.partial(pltpu.with_memory_space_constraint, memory_space=pltpu.HBM)
    msg = front(far(doc_lengths), here, far(features), far(short_taps), far(decay))[0]
    arrived = exchange(msg)
    local = kernel(
        local_body,
        "local",
        "sshvvv",
        (
            sds((tokens, channels), bf16),
            sds((tokens, channels), f32),
            sds((SUB, channels), f32),
            sds((4 * states + 3 * TAPS * groups, LANES), f32),
        ),
        [
            vmem((tokens, LANES), f32),
            vmem(features.shape, bf16),
            vmem((tokens, channels), bf16),
            vmem((HEAD * tokens, tokens), bf16),
            pltpu.SemaphoreType.DMA((3,)),
        ],
        10**8,
        8 * 10**6,
    )
    gate, near, edge, owned = local(doc_lengths, here, far(features), short_taps, decay, residue)
    owner = kernel(
        functools.partial(owner_body, tokens=tokens, modes=modes),
        "owner",
        "svv",
        (sds((blocks, back_rows), bf16),),
        [vmem((out_rows, LANES), f32), vmem((back_rows, LANES), f32)],
        10**6,
        10**6,
    )
    given = exchange(owner(doc_lengths, arrived, owned)[0])
    parts = lax.axis_size("ch")
    join = kernel(
        join_body,
        "join",
        "ssvvvvvvv",
        (sds((tokens, channels), f32), sds((1, tokens), f32)),
        [vmem((back_rows, LANES), f32)],
        10**7,
        5 * 10**6,
    )
    gated, energy = join(doc_lengths, here, given, near, gate, edge, decay, residue, short_taps)
    energy = lax.all_gather(energy, "ch", tiled=True)
    scale = kernel(
        functools.partial(scale_body, width=float(channels * parts)),
        "scale",
        "vvv",
        (sds((tokens, channels), bf16),),
        [vmem((tokens, channels), bf16), pltpu.SemaphoreType.DMA((4,))],
        10**6,
        2 * 10**6,
        pltpu.HBM,
    )
    return scale(energy, gated, gain.reshape(1, channels))[0]


def solution(mesh):
    placed = (
        P(None, ("gr", "gc"), "ch"),
        P(None, None, "ch"),
        P(None, "ch"),
        P(None, "ch"),
        P(),
        P("ch"),
    )
    return jax.shard_map(
        per_device, mesh=mesh, in_specs=placed, out_specs=P(("gr", "gc"), "ch"), check_vma=False
    )
```

```python
import functools

import jax
import jax.numpy as jnp
from jax import lax
from jax.experimental import pallas as pl
from jax.experimental.pallas import tpu as pltpu
from jax.sharding import PartitionSpec as P


LANES = 128
TAPS = 7
HEAD = TAPS - 1
SUB = 8
VMEM_LIMIT = 12 * 1024 * 1024


def doc_start(lengths, position):
    start, found = jnp.int32(0), jnp.zeros_like(position)
    for doc in range(lengths.shape[0]):
        found = jnp.where(position >= start, jnp.maximum(found, start), found)
        start = start + lengths[doc]
    return found


def short_conv(shifts, x, taps):
    tokens = x.shape[0]
    moved = jnp.dot(shifts, x, preferred_element_type=jnp.float32)
    total = x.astype(jnp.float32) * taps(0)
    for i in range(1, TAPS):
        total = total + moved[(i - 1) * tokens : i * tokens] * taps(i)
    return total.astype(jnp.bfloat16)


def rows_of(shape, dim=0):
    return lax.broadcasted_iota(jnp.int32, shape, dim)


def powers(ratio):
    square = ratio * ratio
    fourth = square * square
    return ratio, square, fourth, fourth * fourth


def spread(row, rows=SUB):
    return jnp.broadcast_to(row, (rows, row.shape[1]))


def fill_shifts(shifts, lengths, first_token):
    tokens = shifts.shape[1]
    row = rows_of((tokens, tokens))
    column = rows_of((tokens, tokens), 1)
    position = row + first_token
    reach = position - doc_start(lengths, position)
    for i in range(1, TAPS):
        hit = (column == row - i) & (reach >= i)
        shifts[(i - 1) * tokens : i * tokens, :] = jnp.where(hit, 1.0, 0.0).astype(jnp.bfloat16)


def product_of(first, third):
    product = first.astype(jnp.float32) * third.astype(jnp.float32)
    return jnp.where(rows_of(product.shape) >= HEAD, product, 0.0).astype(jnp.bfloat16)


def front_body(lengths_hbm, here, feats_hbm, taps_hbm, decay_hbm, msg, stage, feats, tail, taps, decay, shifts, lengths, sems):
    pair, tokens, channels = feats.shape
    modes = decay.shape[0]
    groups = channels // LANES
    counted = pltpu.make_async_copy(lengths_hbm, lengths, sems.at[0])
    branches = [pltpu.make_async_copy(feats_hbm.at[2 * k], feats.at[k], sems.at[1 + k]) for k in range(pair)]
    tapped = pltpu.make_async_copy(taps_hbm, taps, sems.at[3])
    others = (
        pltpu.make_async_copy(decay_hbm, decay, sems.at[4]),
        pltpu.make_async_copy(feats_hbm.at[1, tokens - 2 * SUB : tokens, :], tail, sems.at[5]),
    )
    counted.start()
    branches[0].start()
    tapped.start()
    branches[1].start()
    for copy in others:
        copy.start()
    states = groups * modes
    used = states + 5 * HEAD * groups
    if used < stage.shape[0]:
        stage[used:, :] = jnp.zeros((stage.shape[0] - used, LANES), jnp.float32)
    counted.wait()
    fill_shifts(shifts, lengths, here[0] * tokens)
    tapped.wait()
    found = []
    for k in range(pair):
        branches[k].wait()
        found.append(short_conv(shifts[...], feats[k], lambda i, k=k: taps[2 * k, i : i + 1, :]))
    values = product_of(*found).astype(jnp.float32)
    for copy in others:
        copy.wait()
    for j in range(groups):
        mine = slice(j * LANES, (j + 1) * LANES)
        v = values[:, mine]
        tables = powers(jnp.exp(-decay[:, mine]))
        for m in range(modes):
            one, two, four, eight = (spread(t[m : m + 1]) for t in tables)
            state = v[0:SUB]
            for q in range(1, tokens // SUB):
                state = state * eight + v[q * SUB : (q + 1) * SUB]
            state = state * four + pltpu.roll(state, SUB - 4, 0)
            state = state * two + pltpu.roll(state, SUB - 2, 0)
            state = state * one + pltpu.roll(state, SUB - 1, 0)
            stage[j * modes + m : j * modes + m + 1, :] = state[0:1]
        at = states
        last = slice(tokens - 2 * SUB, tokens)
        for part, skip in (
            (feats[0, last, mine], 2 * SUB - HEAD),
            (feats[1, last, mine], 2 * SUB - HEAD),
            (tail[:, mine], 2 * SUB - HEAD),
            (feats[0, 0 : 2 * SUB, mine], 0),
            (feats[1, 0 : 2 * SUB, mine], 0),
        ):
            part = part.astype(jnp.float32)
            for r in range(HEAD):
                stage[at + r * groups + j : at + r * groups + j + 1, :] = part[skip + r : skip + r + 1]
            at += HEAD * groups
    for c in range(stage.shape[0] // LANES):
        msg[:, c * LANES : (c + 1) * LANES] = stage[c * LANES : (c + 1) * LANES, :].T.astype(jnp.bfloat16)


def local_body(
    lengths, here, lane, feats_hbm, taps, decay, residue, gate, near, edge, owned, table, feats, prod, shifts, sems
):
    _, tokens, channels = feats.shape
    modes = decay.shape[0]
    copies = [pltpu.make_async_copy(feats_hbm.at[b], feats.at[b], sems.at[b]) for b in range(3)]
    for copy in copies:
        copy.start()
    fill_shifts(shifts, lengths, here[0] * tokens)
    for copy in copies:
        copy.wait()
    groups = channels // LANES
    chunks = tokens // SUB
    wide = 4 * LANES
    for block in range(channels // wide):
        lanes = slice(block * wide, (block + 1) * wide)
        gate[:, lanes] = short_conv(shifts[...], feats[1, :, lanes], lambda i: taps[1, i : i + 1, lanes])
        prod[:, lanes] = product_of(
            *(
                short_conv(shifts[...], feats[b, :, lanes], lambda i, b=b: taps[b, i : i + 1, lanes])
                for b in (0, 2)
            )
        )
    states = groups * modes
    edge[...] = feats[1, 0 : 2 * SUB, :].astype(jnp.float32)[0:SUB]
    chosen = rows_of((modes, LANES), 1) == lane[0]
    chosen_taps = rows_of((TAPS, LANES), 1) == lane[0]
    for j in range(groups):
        mine = slice(j * LANES, (j + 1) * LANES)
        rates, scale = decay[:, mine], residue[:, mine]
        scale = scale * jnp.sqrt(2.0 * rates)
        pick = jnp.sum(jnp.where(chosen, rates, 0.0), axis=1, keepdims=True)
        pick = jnp.broadcast_to(pick, (modes, LANES))
        for k, count in enumerate((1, tokens - HEAD, tokens)):
            to = k * states + j * modes
            owned[to : to + modes, :] = jnp.exp(-pick * count)
        pick = jnp.sum(jnp.where(chosen, scale, 0.0), axis=1, keepdims=True)
        to = 3 * states + j * modes
        owned[to : to + modes, :] = jnp.broadcast_to(pick, (modes, LANES))
        for b in range(3):
            pick = jnp.sum(jnp.where(chosen_taps, taps[b, :, mine], 0.0), axis=1, keepdims=True)
            pick = jnp.broadcast_to(pick, (TAPS, LANES))
            for i in range(TAPS):
                to = 4 * states + (b * TAPS + i) * groups + j
                owned[to : to + 1, :] = pick[i : i + 1]
    inside = rows_of((SUB, LANES))
    steps = inside.astype(jnp.float32)

    def group(j, carry):
        mine = pl.ds(pl.multiple_of(j * LANES, LANES), LANES)
        sums = [jnp.zeros((SUB, LANES), jnp.float32) for _ in range(chunks)]
        rates = decay[:, mine]
        weights = residue[:, mine] * jnp.sqrt(2.0 * rates)
        eights = jnp.exp(-SUB * rates)
        for m in range(modes):
            step = spread(eights[m : m + 1])
            wave = weights[m : m + 1] * jnp.exp(-rates[m : m + 1] * steps)
            for q in range(chunks):
                sums[q] = sums[q] + wave
                if q + 1 < chunks:
                    wave = wave * step
        for q in range(chunks):
            table[q * SUB : (q + 1) * SUB, :] = sums[q]
        values = prod[:, mine].astype(jnp.float32)
        total = [jnp.zeros((SUB, LANES), jnp.float32) for _ in range(chunks)]
        for k in range(SUB):
            if k:
                turned = [
                    pltpu.roll(values[q * SUB : (q + 1) * SUB], k, 0) for q in range(chunks)
                ]
                low = inside < k
                moved = [
                    jnp.where(low, turned[q - 1] if q else 0.0, turned[q]) for q in range(chunks)
                ]
            else:
                moved = [values[q * SUB : (q + 1) * SUB] for q in range(chunks)]
            for d in range(chunks):
                factor = jnp.broadcast_to(table[d * SUB + k : d * SUB + k + 1, :], (SUB, LANES))
                for q in range(d, chunks):
                    total[q] = total[q] + factor * moved[q - d]
        for q in range(chunks):
            near[q * SUB : (q + 1) * SUB, mine] = total[q]
        return carry

    lax.fori_loop(0, groups, group, 0)


def owner_body(lengths, arrived, owned, back, stage, out, *, tokens, modes):
    blocks = arrived.shape[0]
    groups = owned.shape[0] // (4 * modes + 3 * TAPS)
    states = modes * groups
    for c in range(stage.shape[0] // LANES):
        stage[c * LANES : (c + 1) * LANES, :] = arrived[:, c * LANES : (c + 1) * LANES].astype(jnp.float32).T
    lane = rows_of((groups, blocks), 1)

    def part(k, r):
        at = states + (k * HEAD + r) * groups
        return stage[at : at + groups, :]

    def before(k, r):
        return jnp.where(lane >= 1, pltpu.roll(part(k, r), 1, 1), 0.0)

    reach = []
    for r in range(HEAD):
        position = lane * tokens + r
        reach.append(position - doc_start(lengths, position))
    heads = []
    for last, first, b in ((0, 3, 0), (1, 4, 2)):
        ext = [before(last, r) for r in range(HEAD)] + [part(first, r) for r in range(HEAD)]
        found = []
        for r in range(HEAD):
            total = jnp.zeros((groups, blocks), jnp.float32)
            for i in range(TAPS):
                at = 4 * states + (b * TAPS + i) * groups
                term = owned[at : at + groups, :] * ext[HEAD + r - i]
                total = total + jnp.where(reach[r] >= i, term, 0.0)
            found.append(total.astype(jnp.bfloat16).astype(jnp.float32))
        heads.append(found)
    products = [(a * b).astype(jnp.bfloat16).astype(jnp.float32) for a, b in zip(*heads)]
    lane = rows_of((modes, blocks), 1)
    for j in range(groups):
        at = slice(j * modes, (j + 1) * modes)
        ratio, distant, decline, weight = (
            owned[k * states + j * modes : k * states + (j + 1) * modes, :] for k in range(4)
        )
        rows = [spread(p[j : j + 1], modes) for p in products]
        head = rows[0]
        for r in range(1, HEAD):
            head = head * ratio + rows[r]
        total = stage[at, :] + distant * head
        distance = 1
        while distance < blocks:
            shifted = jnp.where(lane >= distance, pltpu.roll(total, distance, 1), 0.0)
            total = total + decline * shifted
            decline = decline * decline
            distance *= 2
        state = jnp.where(lane >= 1, pltpu.roll(total, 1, 1), 0.0)
        for r in range(HEAD):
            state = state * ratio + rows[r]
            to = states + r * groups + j
            out[to : to + 1, :] = jnp.sum(state * weight, axis=0, keepdims=True)
        out[at, :] = state
    at = states + HEAD * groups
    for r in range(HEAD):
        out[at + r * groups : at + (r + 1) * groups, :] = before(2, r)
    used = states + 2 * HEAD * groups
    if used < out.shape[0]:
        out[used:, :] = jnp.zeros((out.shape[0] - used, LANES), jnp.float32)
    for c in range(out.shape[0] // LANES):
        back[:, c * LANES : (c + 1) * LANES] = out[c * LANES : (c + 1) * LANES, :].T.astype(jnp.bfloat16)


def join_body(lengths, here, back, near, gate, edge, decay, residue, taps, gated, energy, stage):
    tokens, channels = near.shape
    modes = decay.shape[0]
    groups = channels // LANES
    chunks = tokens // SUB
    states = groups * modes
    for c in range(stage.shape[0] // LANES):
        stage[c * LANES : (c + 1) * LANES, :] = back[:, c * LANES : (c + 1) * LANES].astype(jnp.float32).T
    inside = rows_of((SUB, LANES))
    position = inside + here[0] * tokens
    reach = position - doc_start(lengths, position)
    odd, pair, quad = ((inside & bit) != 0 for bit in (1, 2, 4))
    squares = [jnp.zeros((SUB, LANES), jnp.float32) for _ in range(chunks)]
    for j in range(groups):
        mine = slice(j * LANES, (j + 1) * LANES)
        total = [near[q * SUB : (q + 1) * SUB, mine] for q in range(chunks)]
        rates = decay[:, mine]
        tables = powers(jnp.exp(-rates))
        start = stage[j * modes : (j + 1) * modes, :] * residue[:, mine] * jnp.sqrt(2.0 * rates)
        start = start * tables[0] * tables[1]
        grown = jnp.exp(SUB * rates)
        for m in range(modes):
            one, two, four, eight = (spread(t[m : m + 1]) for t in tables)
            wave = spread(start[m : m + 1])
            wave = jnp.where(odd, wave * one, wave)
            wave = jnp.where(pair, wave * two, wave)
            wave = jnp.where(quad, wave * four, wave)
            total[0] = total[0] + wave * spread(grown[m : m + 1])
            for q in range(1, chunks):
                total[q] = total[q] + wave
                if q + 1 < chunks:
                    wave = wave * eight
        told = stage[pl.ds(states + j, SUB, stride=groups), :]
        total[0] = jnp.where(inside < HEAD, told, total[0])
        before = stage[pl.ds(states + HEAD * groups + j, SUB, stride=groups), :]
        now = edge[:, mine]
        front = now * taps[1, 0:1, mine]
        for i in range(1, TAPS):
            moved = jnp.where(inside < i, pltpu.roll(before, (SUB - HEAD + i) % SUB, 0), pltpu.roll(now, i, 0))
            front = front + jnp.where(reach >= i, moved * taps[1, i : i + 1, mine], 0.0)
        front = front.astype(jnp.bfloat16).astype(jnp.float32)
        gates = gate[:, mine].astype(jnp.float32)
        for q in range(chunks):
            g = gates[q * SUB : (q + 1) * SUB] if q else front
            value = g * total[q].astype(jnp.bfloat16).astype(jnp.float32)
            gated[q * SUB : (q + 1) * SUB, mine] = value
            squares[q] = squares[q] + value * value
    summed = jnp.sum(jnp.concatenate(squares, axis=0), axis=1, keepdims=True)
    energy[...] = jnp.broadcast_to(summed, (tokens, LANES)).T[0:1, :]


def scale_body(energy, gated, gain, mixed_hbm, mixed, sems, *, width):
    tokens, channels = gated.shape
    pieces = sems.shape[0]
    rows = tokens // pieces
    scaling = lax.rsqrt(jnp.sum(energy[...], axis=0, keepdims=True) / width + 1e-06)
    scaling = jnp.broadcast_to(scaling, (LANES, tokens)).T
    copies = []
    for k in range(pieces):
        part = slice(k * rows, (k + 1) * rows)
        for j in range(channels // LANES):
            mine = slice(j * LANES, (j + 1) * LANES)
            mixed[part, mine] = (gated[part, mine] * scaling[part] * gain[:, mine]).astype(jnp.bfloat16)
        copies.append(pltpu.make_async_copy(mixed.at[part, :], mixed_hbm.at[part, :], sems.at[k]))
        copies[k].start()
    for copy in copies:
        copy.wait()


def exchange(block, outward):
    blocks, width = block.shape
    slow, fast = lax.axis_size("gr"), lax.axis_size("gc")
    half = width // 2
    if not outward:
        block = block.reshape(slow, fast, 2, half).transpose(1, 0, 2, 3)
    moved = lax.all_to_all(
        block.reshape(blocks, 2, half), ("gc", "gr"), split_axis=0, concat_axis=0, tiled=True
    )
    if outward:
        moved = moved.reshape(fast, slow, 2, half).transpose(1, 0, 2, 3)
    return moved.reshape(blocks, width)


def padded(rows):
    return -(-rows // (2 * LANES)) * 2 * LANES


def kernel(body, name, kinds, outs, scratch, flops, moved, to=pltpu.VMEM):
    spaces = {"s": pltpu.SMEM, "v": pltpu.VMEM, "h": pltpu.HBM}
    return pl.pallas_call(
        body,
        out_shape=outs,
        in_specs=[pl.BlockSpec(memory_space=spaces[k]) for k in kinds],
        out_specs=tuple(pl.BlockSpec(memory_space=to) for _ in outs),
        scratch_shapes=scratch,
        compiler_params=pltpu.CompilerParams(vmem_limit_bytes=VMEM_LIMIT),
        cost_estimate=pl.CostEstimate(flops=flops, bytes_accessed=moved, transcendentals=0),
        name=name,
    )


def per_device(features, short_taps, decay, residue, doc_lengths, gain):
    _, tokens, channels = features.shape
    modes = decay.shape[0]
    blocks = lax.axis_size(("gr", "gc"))
    groups = channels // LANES
    states = groups * modes
    here = lax.axis_index(("gr", "gc")).astype(jnp.int32).reshape(1)
    lane = lax.axis_index(("gc", "gr")).astype(jnp.int32).reshape(1)
    f32, bf16 = jnp.float32, jnp.bfloat16
    sds = jax.ShapeDtypeStruct
    vmem = pltpu.VMEM
    out_rows = padded(states + 5 * HEAD * groups)
    back_rows = padded(states + 2 * HEAD * groups)
    front = kernel(
        front_body,
        "front",
        "hshhh",
        (sds((blocks, out_rows), bf16),),
        [
            vmem((out_rows, LANES), f32),
            vmem((2, tokens, channels), bf16),
            vmem((2 * SUB, channels), bf16),
            vmem(short_taps.shape, f32),
            vmem(decay.shape, f32),
            vmem((HEAD * tokens, tokens), bf16),
            pltpu.SMEM(doc_lengths.shape, jnp.int32),
            pltpu.SemaphoreType.DMA((6,)),
        ],
        10**7,
        4 * 10**6,
    )
    far = functools.partial(pltpu.with_memory_space_constraint, memory_space=pltpu.HBM)
    msg = front(far(doc_lengths), here, far(features), far(short_taps), far(decay))[0]
    arrived = exchange(msg, True)
    local = kernel(
        local_body,
        "local",
        "ssshvvv",
        (
            sds((tokens, channels), bf16),
            sds((tokens, channels), f32),
            sds((SUB, channels), f32),
            sds((4 * states + 3 * TAPS * groups, LANES), f32),
        ),
        [
            vmem((tokens, LANES), f32),
            vmem(features.shape, bf16),
            vmem((tokens, channels), bf16),
            vmem((HEAD * tokens, tokens), bf16),
            pltpu.SemaphoreType.DMA((3,)),
        ],
        10**8,
        8 * 10**6,
    )
    gate, near, edge, owned = local(doc_lengths, here, lane, far(features), short_taps, decay, residue)
    owner = kernel(
        functools.partial(owner_body, tokens=tokens, modes=modes),
        "owner",
        "svv",
        (sds((blocks, back_rows), bf16),),
        [vmem((out_rows, LANES), f32), vmem((back_rows, LANES), f32)],
        10**6,
        10**6,
    )
    given = exchange(owner(doc_lengths, arrived, owned)[0], False)
    parts = lax.axis_size("ch")
    join = kernel(
        join_body,
        "join",
        "ssvvvvvvv",
        (sds((tokens, channels), f32), sds((1, tokens), f32)),
        [vmem((back_rows, LANES), f32)],
        10**7,
        5 * 10**6,
    )
    gated, energy = join(doc_lengths, here, given, near, gate, edge, decay, residue, short_taps)
    energy = lax.all_gather(energy, "ch", tiled=True)
    scale = kernel(
        functools.partial(scale_body, width=float(channels * parts)),
        "scale",
        "vvv",
        (sds((tokens, channels), bf16),),
        [vmem((tokens, channels), bf16), pltpu.SemaphoreType.DMA((4,))],
        10**6,
        2 * 10**6,
        pltpu.HBM,
    )
    return scale(energy, gated, gain.reshape(1, channels))[0]


def solution(mesh):
    placed = (
        P(None, ("gr", "gc"), "ch"),
        P(None, None, "ch"),
        P(None, "ch"),
        P(None, "ch"),
        P(),
        P("ch"),
    )
    return jax.shard_map(
        per_device, mesh=mesh, in_specs=placed, out_specs=P(("gr", "gc"), "ch"), check_vma=False
    )
```

```python
import functools

import jax
import jax.numpy as jnp
from jax import lax
from jax.experimental import pallas as pl
from jax.experimental.pallas import tpu as pltpu
from jax.sharding import PartitionSpec as P


LANES = 128
TAPS = 7
HEAD = TAPS - 1
HALF = HEAD // 2
SUB = 8
VMEM_LIMIT = 12 * 1024 * 1024


def doc_start(lengths, position):
    start, found = jnp.int32(0), jnp.zeros_like(position)
    for doc in range(lengths.shape[0]):
        found = jnp.where(position >= start, jnp.maximum(found, start), found)
        start = start + lengths[doc]
    return found


def short_conv(shifts, x, taps):
    tokens = x.shape[0]
    moved = jnp.dot(shifts, x, preferred_element_type=jnp.float32)
    total = x.astype(jnp.float32) * taps(0)
    for i in range(1, TAPS):
        total = total + moved[(i - 1) * tokens : i * tokens] * taps(i)
    return total.astype(jnp.bfloat16)


def rows_of(shape, dim=0):
    return lax.broadcasted_iota(jnp.int32, shape, dim)


def powers(ratio):
    square = ratio * ratio
    fourth = square * square
    return ratio, square, fourth, fourth * fourth


def spread(row, rows=SUB):
    return jnp.broadcast_to(row, (rows, row.shape[1]))


def fill_shifts(shifts, lengths, first_token):
    count, tokens = shifts.shape
    row = rows_of((tokens, tokens))
    column = rows_of((tokens, tokens), 1)
    position = row + first_token
    reach = position - doc_start(lengths, position)
    for i in range(1, count // tokens + 1):
        hit = (column == row - i) & (reach >= i)
        shifts[(i - 1) * tokens : i * tokens, :] = jnp.where(hit, 1.0, 0.0).astype(jnp.bfloat16)


def mixed_conv(shifts, masks, padded_x, x, taps):
    tokens, width = x.shape
    moved = jnp.dot(shifts[0 : HALF * tokens, :], x, preferred_element_type=jnp.float32)
    found = []
    for g in range(width // LANES):
        mine = slice(g * LANES, (g + 1) * LANES)
        values = x[:, mine].astype(jnp.float32)
        padded_x[g, SUB : SUB + tokens, :] = values
        total = values * taps(0)[:, mine]
        for i in range(1, TAPS):
            if i <= HALF:
                term = moved[(i - 1) * tokens : i * tokens, mine] * taps(i)[:, mine]
            else:
                at = (i - HALF - 1) * tokens
                term = padded_x[g, SUB - i : SUB - i + tokens, :] * taps(i)[:, mine] * masks[at : at + tokens, :]
            total = total + term
        found.append(total)
    return jnp.concatenate(found, axis=1).astype(jnp.bfloat16)


def product_of(first, third):
    product = first.astype(jnp.float32) * third.astype(jnp.float32)
    return jnp.where(rows_of(product.shape) >= HEAD, product, 0.0).astype(jnp.bfloat16)


def front_body(
    lengths_hbm, here, feats_hbm, taps_hbm, decay_hbm, msg, stage, feats, tail, taps, decay, shifts, masks, wide, lengths, sems
):
    pair, tokens, channels = feats.shape
    modes = decay.shape[0]
    groups = channels // LANES
    counted = pltpu.make_async_copy(lengths_hbm, lengths, sems.at[0])
    branches = [pltpu.make_async_copy(feats_hbm.at[2 * k], feats.at[k], sems.at[1 + k]) for k in range(pair)]
    tapped = pltpu.make_async_copy(taps_hbm, taps, sems.at[3])
    others = (
        pltpu.make_async_copy(decay_hbm, decay, sems.at[4]),
        pltpu.make_async_copy(feats_hbm.at[1, tokens - 2 * SUB : tokens, :], tail, sems.at[5]),
    )
    counted.start()
    branches[0].start()
    tapped.start()
    branches[1].start()
    for copy in others:
        copy.start()
    states = groups * modes
    used = states + 5 * HEAD * groups
    if used < stage.shape[0]:
        stage[used:, :] = jnp.zeros((stage.shape[0] - used, LANES), jnp.float32)
    wide[:, :, 0:SUB, :] = jnp.zeros((pair, groups, SUB, LANES), jnp.float32)
    counted.wait()
    fill_shifts(shifts, lengths, here[0] * tokens)
    row = rows_of((tokens, LANES))
    position = row + here[0] * tokens
    reach = jnp.minimum(position - doc_start(lengths, position), row)
    for i in range(HALF + 1, TAPS):
        at = (i - HALF - 1) * tokens
        masks[at : at + tokens, :] = jnp.where(reach >= i, 1.0, 0.0)
    tapped.wait()
    found = []
    for k in range(pair):
        branches[k].wait()
        found.append(
            mixed_conv(shifts, masks, wide.at[k], feats[k], lambda i, k=k: taps[2 * k, i : i + 1, :])
        )
    values = product_of(*found).astype(jnp.float32)
    for copy in others:
        copy.wait()
    for j in range(groups):
        mine = slice(j * LANES, (j + 1) * LANES)
        v = values[:, mine]
        tables = powers(jnp.exp(-decay[:, mine]))
        for m in range(modes):
            one, two, four, eight = (spread(t[m : m + 1]) for t in tables)
            state = v[0:SUB]
            for q in range(1, tokens // SUB):
                state = state * eight + v[q * SUB : (q + 1) * SUB]
            state = state * four + pltpu.roll(state, SUB - 4, 0)
            state = state * two + pltpu.roll(state, SUB - 2, 0)
            state = state * one + pltpu.roll(state, SUB - 1, 0)
            stage[j * modes + m : j * modes + m + 1, :] = state[0:1]
        at = states
        last = slice(tokens - 2 * SUB, tokens)
        for part, skip in (
            (feats[0, last, mine], 2 * SUB - HEAD),
            (feats[1, last, mine], 2 * SUB - HEAD),
            (tail[:, mine], 2 * SUB - HEAD),
            (feats[0, 0 : 2 * SUB, mine], 0),
            (feats[1, 0 : 2 * SUB, mine], 0),
        ):
            part = part.astype(jnp.float32)
            for r in range(HEAD):
                stage[at + r * groups + j : at + r * groups + j + 1, :] = part[skip + r : skip + r + 1]
            at += HEAD * groups
    for c in range(stage.shape[0] // LANES):
        msg[:, c * LANES : (c + 1) * LANES] = stage[c * LANES : (c + 1) * LANES, :].T.astype(jnp.bfloat16)


def local_body(
    lengths, here, feats_hbm, taps, decay, residue, gate, near, edge, owned, table, feats, prod, shifts, sems
):
    _, tokens, channels = feats.shape
    modes = decay.shape[0]
    copies = [pltpu.make_async_copy(feats_hbm.at[b], feats.at[b], sems.at[b]) for b in range(3)]
    for copy in copies:
        copy.start()
    fill_shifts(shifts, lengths, here[0] * tokens)
    for copy in copies:
        copy.wait()
    groups = channels // LANES
    chunks = tokens // SUB
    wide = 4 * LANES
    for block in range(channels // wide):
        lanes = slice(block * wide, (block + 1) * wide)
        gate[:, lanes] = short_conv(shifts[...], feats[1, :, lanes], lambda i: taps[1, i : i + 1, lanes])
        prod[:, lanes] = product_of(
            *(
                short_conv(shifts[...], feats[b, :, lanes], lambda i, b=b: taps[b, i : i + 1, lanes])
                for b in (0, 2)
            )
        )
    states = groups * modes
    edge[...] = feats[1, 0 : 2 * SUB, :].astype(jnp.float32)[0:SUB]
    chosen = rows_of((modes, LANES), 1) == here[0]
    chosen_taps = rows_of((TAPS, LANES), 1) == here[0]
    for j in range(groups):
        mine = slice(j * LANES, (j + 1) * LANES)
        rates, scale = decay[:, mine], residue[:, mine]
        scale = scale * jnp.sqrt(2.0 * rates)
        pick = jnp.sum(jnp.where(chosen, rates, 0.0), axis=1, keepdims=True)
        pick = jnp.broadcast_to(pick, (modes, LANES))
        for k, count in enumerate((1, tokens - HEAD, tokens)):
            to = k * states + j * modes
            owned[to : to + modes, :] = jnp.exp(-pick * count)
        pick = jnp.sum(jnp.where(chosen, scale, 0.0), axis=1, keepdims=True)
        to = 3 * states + j * modes
        owned[to : to + modes, :] = jnp.broadcast_to(pick, (modes, LANES))
        for b in range(3):
            pick = jnp.sum(jnp.where(chosen_taps, taps[b, :, mine], 0.0), axis=1, keepdims=True)
            pick = jnp.broadcast_to(pick, (TAPS, LANES))
            for i in range(TAPS):
                to = 4 * states + (b * TAPS + i) * groups + j
                owned[to : to + 1, :] = pick[i : i + 1]
    inside = rows_of((SUB, LANES))
    steps = inside.astype(jnp.float32)

    def group(j, carry):
        mine = pl.ds(pl.multiple_of(j * LANES, LANES), LANES)
        sums = [jnp.zeros((SUB, LANES), jnp.float32) for _ in range(chunks)]
        rates = decay[:, mine]
        weights = residue[:, mine] * jnp.sqrt(2.0 * rates)
        eights = jnp.exp(-SUB * rates)
        for m in range(modes):
            step = spread(eights[m : m + 1])
            wave = weights[m : m + 1] * jnp.exp(-rates[m : m + 1] * steps)
            for q in range(chunks):
                sums[q] = sums[q] + wave
                if q + 1 < chunks:
                    wave = wave * step
        for q in range(chunks):
            table[q * SUB : (q + 1) * SUB, :] = sums[q]
        values = prod[:, mine].astype(jnp.float32)
        total = [jnp.zeros((SUB, LANES), jnp.float32) for _ in range(chunks)]
        for k in range(SUB):
            if k:
                turned = [
                    pltpu.roll(values[q * SUB : (q + 1) * SUB], k, 0) for q in range(chunks)
                ]
                low = inside < k
                moved = [
                    jnp.where(low, turned[q - 1] if q else 0.0, turned[q]) for q in range(chunks)
                ]
            else:
                moved = [values[q * SUB : (q + 1) * SUB] for q in range(chunks)]
            for d in range(chunks):
                factor = jnp.broadcast_to(table[d * SUB + k : d * SUB + k + 1, :], (SUB, LANES))
                for q in range(d, chunks):
                    total[q] = total[q] + factor * moved[q - d]
        for q in range(chunks):
            near[q * SUB : (q + 1) * SUB, mine] = total[q]
        return carry

    lax.fori_loop(0, groups, group, 0)


def owner_body(lengths, arrived, owned, back, stage, out, *, tokens, modes):
    blocks = arrived.shape[0]
    groups = owned.shape[0] // (4 * modes + 3 * TAPS)
    states = modes * groups
    for c in range(stage.shape[0] // LANES):
        stage[c * LANES : (c + 1) * LANES, :] = arrived[:, c * LANES : (c + 1) * LANES].astype(jnp.float32).T
    lane = rows_of((groups, blocks), 1)

    def part(k, r):
        at = states + (k * HEAD + r) * groups
        return stage[at : at + groups, :]

    def before(k, r):
        return jnp.where(lane >= 1, pltpu.roll(part(k, r), 1, 1), 0.0)

    reach = []
    for r in range(HEAD):
        position = lane * tokens + r
        reach.append(position - doc_start(lengths, position))
    heads = []
    for last, first, b in ((0, 3, 0), (1, 4, 2)):
        ext = [before(last, r) for r in range(HEAD)] + [part(first, r) for r in range(HEAD)]
        found = []
        for r in range(HEAD):
            total = jnp.zeros((groups, blocks), jnp.float32)
            for i in range(TAPS):
                at = 4 * states + (b * TAPS + i) * groups
                term = owned[at : at + groups, :] * ext[HEAD + r - i]
                total = total + jnp.where(reach[r] >= i, term, 0.0)
            found.append(total.astype(jnp.bfloat16).astype(jnp.float32))
        heads.append(found)
    products = [(a * b).astype(jnp.bfloat16).astype(jnp.float32) for a, b in zip(*heads)]
    lane = rows_of((modes, blocks), 1)
    for j in range(groups):
        at = slice(j * modes, (j + 1) * modes)
        ratio, distant, decline, weight = (
            owned[k * states + j * modes : k * states + (j + 1) * modes, :] for k in range(4)
        )
        rows = [spread(p[j : j + 1], modes) for p in products]
        head = rows[0]
        for r in range(1, HEAD):
            head = head * ratio + rows[r]
        total = stage[at, :] + distant * head
        distance = 1
        while distance < blocks:
            shifted = jnp.where(lane >= distance, pltpu.roll(total, distance, 1), 0.0)
            total = total + decline * shifted
            decline = decline * decline
            distance *= 2
        state = jnp.where(lane >= 1, pltpu.roll(total, 1, 1), 0.0)
        for r in range(HEAD):
            state = state * ratio + rows[r]
            to = states + r * groups + j
            out[to : to + 1, :] = jnp.sum(state * weight, axis=0, keepdims=True)
        out[at, :] = state
    at = states + HEAD * groups
    for r in range(HEAD):
        out[at + r * groups : at + (r + 1) * groups, :] = before(2, r)
    used = states + 2 * HEAD * groups
    if used < out.shape[0]:
        out[used:, :] = jnp.zeros((out.shape[0] - used, LANES), jnp.float32)
    for c in range(out.shape[0] // LANES):
        back[:, c * LANES : (c + 1) * LANES] = out[c * LANES : (c + 1) * LANES, :].T.astype(jnp.bfloat16)


def join_body(lengths, here, back, near, gate, edge, decay, residue, taps, gated, energy, stage):
    tokens, channels = near.shape
    modes = decay.shape[0]
    groups = channels // LANES
    chunks = tokens // SUB
    states = groups * modes
    for c in range(stage.shape[0] // LANES):
        stage[c * LANES : (c + 1) * LANES, :] = back[:, c * LANES : (c + 1) * LANES].astype(jnp.float32).T
    inside = rows_of((SUB, LANES))
    position = inside + here[0] * tokens
    reach = position - doc_start(lengths, position)
    odd, pair, quad = ((inside & bit) != 0 for bit in (1, 2, 4))
    squares = [jnp.zeros((SUB, LANES), jnp.float32) for _ in range(chunks)]
    for j in range(groups):
        mine = slice(j * LANES, (j + 1) * LANES)
        total = [near[q * SUB : (q + 1) * SUB, mine] for q in range(chunks)]
        rates = decay[:, mine]
        tables = powers(jnp.exp(-rates))
        start = stage[j * modes : (j + 1) * modes, :] * residue[:, mine] * jnp.sqrt(2.0 * rates)
        start = start * tables[0] * tables[1]
        grown = jnp.exp(SUB * rates)
        for m in range(modes):
            one, two, four, eight = (spread(t[m : m + 1]) for t in tables)
            wave = spread(start[m : m + 1])
            wave = jnp.where(odd, wave * one, wave)
            wave = jnp.where(pair, wave * two, wave)
            wave = jnp.where(quad, wave * four, wave)
            total[0] = total[0] + wave * spread(grown[m : m + 1])
            for q in range(1, chunks):
                total[q] = total[q] + wave
                if q + 1 < chunks:
                    wave = wave * eight
        told = stage[pl.ds(states + j, SUB, stride=groups), :]
        total[0] = jnp.where(inside < HEAD, told, total[0])
        before = stage[pl.ds(states + HEAD * groups + j, SUB, stride=groups), :]
        now = edge[:, mine]
        front = now * taps[1, 0:1, mine]
        for i in range(1, TAPS):
            moved = jnp.where(inside < i, pltpu.roll(before, (SUB - HEAD + i) % SUB, 0), pltpu.roll(now, i, 0))
            front = front + jnp.where(reach >= i, moved * taps[1, i : i + 1, mine], 0.0)
        front = front.astype(jnp.bfloat16).astype(jnp.float32)
        gates = gate[:, mine].astype(jnp.float32)
        for q in range(chunks):
            g = gates[q * SUB : (q + 1) * SUB] if q else front
            value = g * total[q].astype(jnp.bfloat16).astype(jnp.float32)
            gated[q * SUB : (q + 1) * SUB, mine] = value
            squares[q] = squares[q] + value * value
    summed = jnp.sum(jnp.concatenate(squares, axis=0), axis=1, keepdims=True)
    energy[...] = jnp.broadcast_to(summed, (tokens, LANES)).T[0:1, :]


def scale_body(energy, gated, gain, mixed_hbm, mixed, sems, *, width):
    tokens, channels = gated.shape
    pieces = sems.shape[0]
    rows = tokens // pieces
    scaling = lax.rsqrt(jnp.sum(energy[...], axis=0, keepdims=True) / width + 1e-06)
    scaling = jnp.broadcast_to(scaling, (LANES, tokens)).T
    copies = []
    for k in range(pieces):
        part = slice(k * rows, (k + 1) * rows)
        for j in range(channels // LANES):
            mine = slice(j * LANES, (j + 1) * LANES)
            mixed[part, mine] = (gated[part, mine] * scaling[part] * gain[:, mine]).astype(jnp.bfloat16)
        copies.append(pltpu.make_async_copy(mixed.at[part, :], mixed_hbm.at[part, :], sems.at[k]))
        copies[k].start()
    for copy in copies:
        copy.wait()


def exchange(block):
    blocks, width = block.shape
    moved = lax.all_to_all(
        block.reshape(blocks, 2, width // 2), ("gr", "gc"), split_axis=0, concat_axis=0, tiled=True
    )
    return moved.reshape(blocks, width)


def padded(rows):
    return -(-rows // (2 * LANES)) * 2 * LANES


def kernel(body, name, kinds, outs, scratch, flops, moved, to=pltpu.VMEM):
    spaces = {"s": pltpu.SMEM, "v": pltpu.VMEM, "h": pltpu.HBM}
    return pl.pallas_call(
        body,
        out_shape=outs,
        in_specs=[pl.BlockSpec(memory_space=spaces[k]) for k in kinds],
        out_specs=tuple(pl.BlockSpec(memory_space=to) for _ in outs),
        scratch_shapes=scratch,
        compiler_params=pltpu.CompilerParams(vmem_limit_bytes=VMEM_LIMIT),
        cost_estimate=pl.CostEstimate(flops=flops, bytes_accessed=moved, transcendentals=0),
        name=name,
    )


def per_device(features, short_taps, decay, residue, doc_lengths, gain):
    _, tokens, channels = features.shape
    modes = decay.shape[0]
    blocks = lax.axis_size(("gr", "gc"))
    groups = channels // LANES
    states = groups * modes
    here = lax.axis_index(("gr", "gc")).astype(jnp.int32).reshape(1)
    f32, bf16 = jnp.float32, jnp.bfloat16
    sds = jax.ShapeDtypeStruct
    vmem = pltpu.VMEM
    out_rows = padded(states + 5 * HEAD * groups)
    back_rows = padded(states + 2 * HEAD * groups)
    front = kernel(
        front_body,
        "front",
        "hshhh",
        (sds((blocks, out_rows), bf16),),
        [
            vmem((out_rows, LANES), f32),
            vmem((2, tokens, channels), bf16),
            vmem((2 * SUB, channels), bf16),
            vmem(short_taps.shape, f32),
            vmem(decay.shape, f32),
            vmem((HALF * tokens, tokens), bf16),
            vmem(((HEAD - HALF) * tokens, LANES), f32),
            vmem((2, groups, SUB + tokens, LANES), f32),
            pltpu.SMEM(doc_lengths.shape, jnp.int32),
            pltpu.SemaphoreType.DMA((6,)),
        ],
        10**7,
        4 * 10**6,
    )
    far = functools.partial(pltpu.with_memory_space_constraint, memory_space=pltpu.HBM)
    msg = front(far(doc_lengths), here, far(features), far(short_taps), far(decay))[0]
    arrived = exchange(msg)
    local = kernel(
        local_body,
        "local",
        "sshvvv",
        (
            sds((tokens, channels), bf16),
            sds((tokens, channels), f32),
            sds((SUB, channels), f32),
            sds((4 * states + 3 * TAPS * groups, LANES), f32),
        ),
        [
            vmem((tokens, LANES), f32),
            vmem(features.shape, bf16),
            vmem((tokens, channels), bf16),
            vmem((HEAD * tokens, tokens), bf16),
            pltpu.SemaphoreType.DMA((3,)),
        ],
        10**8,
        8 * 10**6,
    )
    gate, near, edge, owned = local(doc_lengths, here, far(features), short_taps, decay, residue)
    owner = kernel(
        functools.partial(owner_body, tokens=tokens, modes=modes),
        "owner",
        "svv",
        (sds((blocks, back_rows), bf16),),
        [vmem((out_rows, LANES), f32), vmem((back_rows, LANES), f32)],
        10**6,
        10**6,
    )
    given = exchange(owner(doc_lengths, arrived, owned)[0])
    parts = lax.axis_size("ch")
    join = kernel(
        join_body,
        "join",
        "ssvvvvvvv",
        (sds((tokens, channels), f32), sds((1, tokens), f32)),
        [vmem((back_rows, LANES), f32)],
        10**7,
        5 * 10**6,
    )
    gated, energy = join(doc_lengths, here, given, near, gate, edge, decay, residue, short_taps)
    energy = lax.all_gather(energy, "ch", tiled=True)
    scale = kernel(
        functools.partial(scale_body, width=float(channels * parts)),
        "scale",
        "vvv",
        (sds((tokens, channels), bf16),),
        [vmem((tokens, channels), bf16), pltpu.SemaphoreType.DMA((4,))],
        10**6,
        2 * 10**6,
        pltpu.HBM,
    )
    return scale(energy, gated, gain.reshape(1, channels))[0]


def solution(mesh):
    placed = (
        P(None, ("gr", "gc"), "ch"),
        P(None, None, "ch"),
        P(None, "ch"),
        P(None, "ch"),
        P(),
        P("ch"),
    )
    return jax.shard_map(
        per_device, mesh=mesh, in_specs=placed, out_specs=P(("gr", "gc"), "ch"), check_vma=False
    )
```
